256 devices in a mesh: dom: 16 (over x, z_lo, core), cls: 16 (over y, z_hi).
Axes of the slice: x: 4, y: 4, z: 8 (z_hi: 4, z_lo: 2; z = z_hi * 2 + z_lo), core: 2. Of those that a mesh axis runs over, the one named last changes fastest.
Arguments:
- images: bfloat16 [8192, 128, 256], P(('dom', 'cls')), may hold values from -400 to 400
- defocus: bfloat16 [8192], P(('dom', 'cls')), may hold values from 2 to 20
- assign: int32 [8192], P(('dom', 'cls')), may hold values from 0 to 1
- orient: int32 [8192], P(('dom', 'cls')), may hold values from 0 to 511
- owner: int32 [8192, 16], P(('dom', 'cls')), may hold values from 0 to 15, as said below
- slice_loc: int32 [512, 16], replicated, may hold values from 0 to 127
- volume: bfloat16 [2, 2048, 2048], P(None, 'cls'), may hold values from -6 to 6
Outputs:
- new_volume: float32 [2, 2048, 2048], P(None, 'cls', 'dom')
- correlation: float32 [8192], P(('dom', 'cls'))
The draws below stay inside these ranges and needn't reach their ends.
Inputs may be any that keep to these rules, and one draw needn't show every extreme that they name: `owner`: of the 16 block rows of each of one device's 32 particles, at most 80 together name any one index of cls; in every draw one index is named by exactly 80 of these rows on every device, and on some devices a second index too.
All inputs are finite; a program needn't handle non-finite values.
Results may differ from the reference program's by a relative error of at most 0.0029.
Values may be sent and summed in bfloat16 or wider, within the bound.
No kernel may reach another device: no remote copies, remote signals or barrier semaphores. Data moves between devices by JAX's collectives and lax.ppermute only.
A program may use at most 128 MiB of HBM per device.

```python
import math
import jax
import jax.numpy as jnp
import numpy as np
from jax import lax

R = 128
F = 256
BR = 8
SB = 16
KC = 2
NORI = 512
P_DEV = 32
BLK_DEV = 128
NBLK = 2048
NPART = 8192
CAP = 80
N_CLS = 16


def draw_images(key, part):
    key = jax.random.fold_in(key, 11)
    key_base, key_part, key_row, key_col = jax.random.split(key, 4)
    base = jnp.clip(jax.random.normal(key_base, (NPART, R, F), jnp.float32), -4.0, 4.0)
    part_scale = jnp.exp(jax.random.uniform(key_part, (NPART, 1, 1), jnp.float32, 0.0, math.log(10.0)))
    row_scale = jnp.exp(jax.random.uniform(key_row, (1, R, 1), jnp.float32, 0.0, math.log(3.0)))
    col_scale = jnp.exp(jax.random.uniform(key_col, (1, 1, F), jnp.float32, 0.0, math.log(3.0)))
    return (base * part_scale * row_scale * col_scale).astype(jnp.bfloat16)


def draw_owner(key, part):
    key = jax.random.fold_in(key, 23)
    key_busiest, key_devices = jax.random.split(key)
    row_count = P_DEV * SB
    slot_count = N_CLS * CAP
    device_count = NPART // P_DEV
    busiest = jax.random.randint(key_busiest, (), 0, N_CLS)
    slot_owner = jnp.arange(slot_count, dtype=jnp.int32) // CAP

    def one_device(device_key):
        key_second, key_flag, key_score, key_shuffle = jax.random.split(device_key, 4)
        runner_up = (busiest + jax.random.randint(key_second, (), 1, N_CLS)) % N_CLS
        doubled = jax.random.randint(key_flag, (), 0, 2)
        scores = jax.random.randint(key_score, (slot_count,), 0, 4096)
        priority = jnp.where(slot_owner == busiest, 2, jnp.where(slot_owner == runner_up, doubled, 0))
        ranked = priority * 67108864 + scores * slot_count + jnp.arange(slot_count, dtype=jnp.int32)
        chosen = lax.top_k(ranked, row_count)[1]
        picked = slot_owner[chosen]
        return picked[jax.random.permutation(key_shuffle, row_count)]
    device_keys = jax.random.split(key_devices, device_count)
    return jax.vmap(one_device)(device_keys).reshape(NPART, SB).astype(jnp.int32)


def plant(drawn, key, low, high):
    index_at = [jax.random.randint(jax.random.fold_in(key, axis), (), 0, length) for axis, length in enumerate(drawn.shape)]
    longest = drawn.shape.index(max(drawn.shape))
    beside = index_at[:longest] + [(index_at[longest] + 1) % drawn.shape[longest]] + index_at[longest + 1:]
    return drawn.at[tuple(index_at)].set(low).at[tuple(beside)].set(high)


def block_levels(stream_key, shape, cuts, smallest, top_value):
    gain = 1.0
    for dim, blocks in cuts:
        draws = jax.random.uniform(jax.random.fold_in(jax.random.fold_in(stream_key, 6), dim), (blocks,), jnp.float32, smallest / len(cuts), top_value / len(cuts))
        gain = gain * jnp.repeat(jnp.exp(draws), shape[dim] // blocks).reshape((-1,) + (1,) * (len(shape) - 1 - dim))
    return gain


def rank_table(number_of, skew):
    loads = [(1 << 20) // math.isqrt(rank ** skew) + 1 for rank in range(1, number_of + 1)]
    deviation = 1 + sum(loads) // (1 << 30)
    return np.cumsum(np.array([max(1, weight // deviation) for weight in loads]))


def skewed_ids(own_key, shape, amount, slope):
    grid = rank_table(amount, slope)
    ticket = jax.random.randint(jax.random.fold_in(own_key, 1), shape, 0, int(grid[amount - 1]))
    grade = jnp.searchsorted(jnp.asarray(grid, jnp.int32), ticket, side="right")
    return jax.random.permutation(jax.random.fold_in(own_key, 2), amount)[grade].astype(jnp.int32)


def scatter_about(own_key, dims, deviation, bound, cuts=(), kind=jnp.bfloat16):
    entries = jax.random.normal(own_key, dims, jnp.float32) * deviation
    if len(cuts) > 0:
        entries = block_levels(own_key, dims, cuts, -0.22, 0.18) * entries
    return jnp.clip(entries, min=-bound, max=bound).astype(kind)


def setup_inputs(seed: int = 0) -> dict:
    seeds = jax.random.split(jax.random.key(seed), 8)
    images = draw_images(jax.random.fold_in(seeds[7], 71), 0)
    defocus = jnp.clip(jnp.exp(math.log(20.0) - 2.3025851 * jax.random.uniform(seeds[1], (NPART,), jnp.float32) ** block_levels(seeds[1], (NPART,), ((0, 256),), -0.2, 0.2)), 2.0, 20.0).astype(jnp.bfloat16)
    assign = plant(jax.random.randint(seeds[2], (NPART,), 0, KC), jax.random.fold_in(seeds[2], 1), 0, KC - 1).astype(jnp.int32)
    orient = plant(skewed_ids(seeds[3], (NPART,), NORI, 2), jax.random.fold_in(seeds[3], 3), 0, NORI - 1).astype(jnp.int32)
    owner = draw_owner(jax.random.fold_in(seeds[7], 71), 0)
    slice_loc = plant(jax.random.randint(seeds[5], (NORI, SB), 0, BLK_DEV), jax.random.fold_in(seeds[5], 1), 0, BLK_DEV - 1).astype(jnp.int32)
    volume = scatter_about(seeds[6], (KC, NBLK, BR * F), 1.0, 6.0, ((1, 16),))
    return {"images": images, "defocus": defocus, "assign": assign, "orient": orient, "owner": owner, "slice_loc": slice_loc, "volume": volume}


def wave_radius(row_index, width, extent):
    column = (jnp.arange(width, dtype=jnp.int32) % (width // 2)).astype(jnp.float32)
    row_value = row_index.astype(jnp.float32)
    return (row_value[:, None] * row_value[:, None] + column[None, :] * column[None, :]) / float(extent * extent)

def contrast(defocus, radius):
    return jnp.sin(defocus.astype(jnp.float32)[:, None, None] * radius[None, :, :] + 0.3)

def reference(images, defocus, assign, orient, owner, slice_loc, volume):
    radius = wave_radius(jnp.arange(R, dtype=jnp.int32), F, R)
    flat_volume = volume.reshape(KC * NBLK, BR * F)
    group_size = P_DEV * N_CLS
    group_count = NPART // group_size

    def one_group(carry, pieces):
        numer, denom = carry
        image_block, focus_block, class_block, orient_block, owner_block = pieces
        target = class_block[:, None] * NBLK + owner_block * BLK_DEV + slice_loc[orient_block]
        target = target.astype(jnp.int32)
        ref_rows = flat_volume[target].reshape(group_size, R, F).astype(jnp.float32)
        ctf_map = contrast(focus_block, radius)
        samples = image_block.astype(jnp.float32)
        projected = ctf_map * ref_rows
        cross_sum = lax.optimization_barrier(jnp.sum(projected * samples, axis=(1, 2)))
        power_sum = lax.optimization_barrier(jnp.sum(projected * projected, axis=(1, 2)))
        noise_power = lax.optimization_barrier(jnp.mean(samples * samples, axis=(1, 2))) + 1e-05
        corr_value = cross_sum / jnp.sqrt((power_sum + 1e-05) * noise_power)
        weight = jax.nn.sigmoid(corr_value) / noise_power
        scaled = weight[:, None, None] * ctf_map
        numer_term = lax.optimization_barrier((scaled * samples).astype(jnp.bfloat16))
        denom_term = lax.optimization_barrier((scaled * ctf_map).astype(jnp.bfloat16))
        flat_target = target.reshape(-1)
        numer = numer.at[flat_target].add(numer_term.reshape(group_size * SB, BR * F).astype(jnp.float32))
        denom = denom.at[flat_target].add(denom_term.reshape(group_size * SB, BR * F).astype(jnp.float32))
        return ((numer, denom), corr_value)
    start_numer = jnp.zeros((KC * NBLK, BR * F), jnp.float32)
    start_denom = jnp.zeros((KC * NBLK, BR * F), jnp.float32)
    pieces = (images.reshape(group_count, group_size, R, F), defocus.reshape(group_count, group_size), assign.reshape(group_count, group_size), orient.reshape(group_count, group_size), owner.reshape(group_count, group_size, SB))
    (numer, denom), corr_all = lax.scan(one_group, (start_numer, start_denom), pieces)
    new_volume = (numer / (denom + 1.0)).reshape(KC, NBLK, BR * F)
    return (new_volume, corr_all.reshape(NPART))
```

```python
import functools
import jax
import jax.numpy as jnp
from jax import lax
from jax.experimental import pallas as pl
from jax.experimental.pallas import tpu as pltpu
from jax.sharding import PartitionSpec as P

F32 = jnp.float32
BF16 = jnp.bfloat16
LANES = 128
PHASE = 0.3
EPS = 1e-05
VMEM_LIMIT = 56 * 1024 * 1024


def params(semantics=None):
    return pltpu.CompilerParams(vmem_limit_bytes=VMEM_LIMIT, dimension_semantics=semantics)


def split_kernel(particles, slices, block_rows, img_ref, out_ref, scratch):
    rows = slices * block_rows
    for h in range(2):
        half = img_ref[:, :, h * LANES : (h + 1) * LANES].astype(F32)
        scratch[h] = half.reshape(particles * rows, LANES)
    for j in range(slices):
        for b in range(block_rows):
            picked = pl.ds(j * block_rows + b, particles, stride=rows)
            for h in range(2):
                out_ref[2 * b + h, j] = scratch[h, picked, :].astype(BF16)


def split_images(images, slices):
    particles, rows, width = images.shape
    block_rows = rows // slices
    step = 16
    return pl.pallas_call(
        functools.partial(split_kernel, step, slices, block_rows),
        grid=(particles // step,),
        in_specs=[pl.BlockSpec((step, rows, width), lambda i: (i, 0, 0))],
        out_specs=pl.BlockSpec((2 * block_rows, slices, step, LANES), lambda i: (0, 0, i, 0)),
        out_shape=jax.ShapeDtypeStruct((2 * block_rows, slices, particles, LANES), BF16),
        scratch_shapes=[pltpu.VMEM((2, step * rows, LANES), F32)],
        compiler_params=params(),
        cost_estimate=pl.CostEstimate(flops=0, bytes_accessed=images.size * 8, transcendentals=0),
    )(images)


def project_kernel(
    slices, particles, extent, row_ref, key_ref, focus_ref, vol_ref, proj_ref, ctf_ref, power_ref
):
    count = slices * particles
    key = jnp.broadcast_to(key_ref[0], (8, count)).T[:, :1]
    half = vol_ref.shape[0] // 2
    blocks = vol_ref.shape[1]
    upper = key >= float(half * blocks)
    low = jnp.where(upper, key - float(half * blocks), key)
    low = jnp.broadcast_to(low, (count, blocks))
    lane = lax.broadcasted_iota(jnp.int32, (count, blocks), 1).astype(F32)
    acc = jnp.zeros((count, 2 * LANES), F32)
    for o in range(half):
        one_hot = (low == lane + float(o * blocks)).astype(BF16)
        both = jnp.concatenate([vol_ref[o], vol_ref[o + half]], axis=1)
        acc += jnp.dot(one_hot, both, preferred_element_type=F32)
    picked = jnp.where(
        jnp.broadcast_to(upper, (count, LANES)), acc[:, LANES:], acc[:, :LANES]
    ).reshape(slices, particles, LANES)
    focus = jnp.broadcast_to(focus_ref[0], (8, particles)).T[:, :1]
    focus = jnp.broadcast_to(focus, (particles, LANES)) / extent
    column = lax.broadcasted_iota(jnp.int32, (particles, LANES), 1).astype(F32)
    angle = focus * (column * column)
    cos_col, sin_col = jnp.cos(angle), jnp.sin(angle)
    row = column * 8.0 + row_ref[0]
    angle = focus * (row * row) + PHASE
    cos_row, sin_row = jnp.cos(angle), jnp.sin(angle)
    power = jnp.zeros((particles, LANES), F32)
    for j in range(slices):
        ctf = sin_row[:, j : j + 1] * cos_col + cos_row[:, j : j + 1] * sin_col
        proj = ctf * picked[j]
        power += proj * proj
        ctf_ref[0, j] = ctf
        proj_ref[0, j] = proj
    power_ref[0] = power


def project(row, keys, focus, vol, extent):
    senders, slices, particles = keys.shape
    owners, blocks, _ = vol.shape
    shape = (senders, slices, particles, LANES)
    block = pl.BlockSpec((1, slices, particles, LANES), lambda s: (s, 0, 0, 0))
    return pl.pallas_call(
        functools.partial(project_kernel, slices, particles, extent),
        grid=(senders,),
        in_specs=[
            pl.BlockSpec(memory_space=pltpu.SMEM),
            pl.BlockSpec((1, 1, slices * particles), lambda s: (s, 0, 0)),
            pl.BlockSpec((1, 1, particles), lambda s: (s, 0, 0)),
            pl.BlockSpec((owners, blocks, LANES), lambda s: (0, 0, 0)),
        ],
        out_specs=[block, block, pl.BlockSpec((1, particles, LANES), lambda s: (s, 0, 0))],
        out_shape=[
            jax.ShapeDtypeStruct(shape, F32),
            jax.ShapeDtypeStruct(shape, F32),
            jax.ShapeDtypeStruct((senders, particles, LANES), F32),
        ],
        compiler_params=params(),
        cost_estimate=pl.CostEstimate(
            flops=2 * senders * slices * particles * owners * blocks * LANES,
            bytes_accessed=10 * 1024 * 1024,
            transcendentals=0,
        ),
    )(row, keys.reshape(senders, 1, slices * particles), focus.reshape(senders, 1, particles), vol)


def sums_kernel(slices, particles, img_ref, proj_ref, power_ref, out_ref, cross_acc, noise_acc):
    s = pl.program_id(0)
    cross = jnp.zeros((particles, LANES), F32)
    noise = jnp.zeros((particles, LANES), F32)
    for j in range(slices):
        img = img_ref[0, j].astype(F32)
        cross += img * proj_ref[0, j]
        noise += img * img
    cross_acc[pl.ds(s * particles, particles), :] = cross
    noise_acc[pl.ds(s * particles, particles), :] = noise

    @pl.when(s == pl.num_programs(0) - 1)
    def _():
        total = out_ref.shape[1] // 3
        for i, ref in enumerate((cross_acc, power_ref, noise_acc)):
            out_ref[:, i * total : (i + 1) * total] = jnp.sum(ref[...].T, axis=0, keepdims=True)


def partial_sums(img, proj, power):
    senders, slices, particles, _ = img.shape
    total = senders * particles
    block = pl.BlockSpec((1, slices, particles, LANES), lambda s: (s, 0, 0, 0))
    return pl.pallas_call(
        functools.partial(sums_kernel, slices, particles),
        grid=(senders,),
        in_specs=[block, block, pl.BlockSpec((total, LANES), lambda s: (0, 0))],
        out_specs=pl.BlockSpec((1, 3 * total), lambda s: (0, 0)),
        out_shape=jax.ShapeDtypeStruct((1, 3 * total), F32),
        scratch_shapes=[pltpu.VMEM((total, LANES), F32), pltpu.VMEM((total, LANES), F32)],
        compiler_params=params(),
        cost_estimate=pl.CostEstimate(
            flops=img.size * 4, bytes_accessed=img.size * 6, transcendentals=0
        ),
    )(img, proj, power.reshape(total, LANES))


def terms_kernel(
    slices, particles, pixels, part_ref, img_ref, ctf_ref, terms_ref, corr_ref, weight_col
):
    s = pl.program_id(0)

    @pl.when(s == 0)
    def _():
        total = part_ref.shape[1] // 3
        sums = jnp.sum(part_ref[...], axis=0, keepdims=True)
        cross, power = sums[:, :total], sums[:, total : 2 * total]
        noise = sums[:, 2 * total :] / pixels + EPS
        corr = cross / jnp.sqrt((power + EPS) * noise)
        corr_ref[...] = corr
        weight = jax.nn.sigmoid(corr) / noise
        weight_col[...] = jnp.broadcast_to(weight, (LANES, total)).T

    weight = weight_col[pl.ds(s * particles, particles), :]
    for j in range(slices):
        ctf = ctf_ref[0, j]
        scaled = weight * ctf
        rows = pl.ds(j * particles, particles)
        terms_ref[rows, :LANES] = (scaled * img_ref[0, j].astype(F32)).astype(BF16)
        terms_ref[rows, LANES:] = (scaled * ctf).astype(BF16)


def make_terms(partials, img, ctf):
    senders, slices, particles, _ = img.shape
    total = senders * particles
    block = pl.BlockSpec((1, slices, particles, LANES), lambda s: (s, 0, 0, 0))
    return pl.pallas_call(
        functools.partial(terms_kernel, slices, particles, float(slices * 8 * 2 * LANES)),
        grid=(senders,),
        in_specs=[pl.BlockSpec(partials.shape, lambda s: (0, 0)), block, block],
        out_specs=[
            pl.BlockSpec((slices * particles, 2 * LANES), lambda s: (s, 0)),
            pl.BlockSpec((1, total), lambda s: (0, 0)),
        ],
        out_shape=[
            jax.ShapeDtypeStruct((senders * slices * particles, 2 * LANES), BF16),
            jax.ShapeDtypeStruct((1, total), F32),
        ],
        scratch_shapes=[pltpu.VMEM((total, LANES), F32)],
        compiler_params=params(),
        cost_estimate=pl.CostEstimate(
            flops=img.size * 4, bytes_accessed=img.size * 10, transcendentals=0
        ),
    )(partials, img, ctf)


def scatter_kernel(blocks, first, size, key_ref, terms_ref, out_ref):
    o = pl.program_id(0)
    rows = terms_ref.shape[0]
    base = (o * blocks + first).astype(F32)
    depth = 1024
    acc = jnp.zeros((size, 2 * LANES), F32)
    for i in range(rows // depth):
        key = key_ref[:, i * depth : (i + 1) * depth] - base
        slot = lax.broadcasted_iota(jnp.int32, (size, depth), 0).astype(F32)
        one_hot = (slot == key).astype(BF16)
        acc += jnp.dot(
            one_hot, terms_ref[i * depth : (i + 1) * depth, :], preferred_element_type=F32
        )
    out_ref[0] = acc.astype(BF16)


def scatter(keys, terms, owners, blocks, first, size):
    rows = terms.shape[0]
    return pl.pallas_call(
        functools.partial(scatter_kernel, blocks, first, size),
        grid=(owners,),
        in_specs=[
            pl.BlockSpec((1, rows), lambda o: (0, 0)),
            pl.BlockSpec((rows, 2 * LANES), lambda o: (0, 0)),
        ],
        out_specs=pl.BlockSpec((1, size, 2 * LANES), lambda o: (o, 0, 0)),
        out_shape=jax.ShapeDtypeStruct((owners, size, 2 * LANES), BF16),
        compiler_params=params(),
        cost_estimate=pl.CostEstimate(
            flops=2 * rows * owners * size * 2 * LANES,
            bytes_accessed=terms.size * 2 + owners * size * 512,
            transcendentals=0,
        ),
    )(keys.reshape(1, rows), terms)


def shards(images, defocus, assign, orient, owner, slice_loc, volume):
    owners = lax.axis_size("cls")
    groups = lax.axis_size("dom")
    me = lax.axis_index("dom")
    particles, image_rows, width = images.shape
    classes, owned, block_len = volume.shape
    slices = owner.shape[1]
    blocks = classes * owned
    total = groups * particles

    piece = lax.dynamic_slice_in_dim(volume, me * LANES, LANES, axis=2).reshape(blocks, LANES)
    vol = lax.all_gather(piece, "cls", axis=0, tiled=False)

    place = slice_loc[orient]
    key = (owner * blocks + assign[:, None] * owned + place).astype(F32).T
    meta = jnp.concatenate([key.reshape(-1), defocus.astype(F32)])
    meta = jnp.broadcast_to(meta[None, None, :], (groups, 1, meta.shape[0]))
    meta = lax.all_to_all(meta, "dom", 0, 0, tiled=True)[:, 0, :]
    keys = meta[:, : slices * particles].reshape(groups, slices, particles)
    focus = meta[:, slices * particles :]

    img = split_images(images, slices)
    img = lax.all_to_all(img, "dom", 0, 0, tiled=True)

    row = (me // 2).astype(F32).reshape(1)
    proj, ctf, power = project(row, keys, focus, vol, float(image_rows * image_rows))
    partial = partial_sums(img, proj, power)
    partial = jnp.broadcast_to(partial[None], (groups,) + partial.shape)
    partial = lax.all_to_all(partial, "dom", 0, 0, tiled=True)[:, 0, :]
    terms, corr = make_terms(partial, img, ctf)
    correlation = lax.dynamic_slice_in_dim(corr[0], me * particles, particles)

    volumes = []
    sent = []
    for c in range(classes):
        summed = scatter(keys, terms, owners, blocks, c * owned, owned)
        sent.append(lax.all_to_all(summed, "cls", 0, 0, tiled=True))
    for got in sent:
        whole = jnp.sum(got.astype(F32), axis=0)
        volumes.append(whole[:, :LANES] / (whole[:, LANES:] + 1.0))
    return (jnp.stack(volumes), correlation)


def solution(mesh):
    placed = (
        P(("dom", "cls"), None, None),
        P(("dom", "cls")),
        P(("dom", "cls")),
        P(("dom", "cls")),
        P(("dom", "cls"), None),
        P(),
        P(None, "cls", None),
    )
    return jax.shard_map(
        shards,
        mesh=mesh,
        in_specs=placed,
        out_specs=(P(None, "cls", "dom"), P(("dom", "cls"))),
        check_vma=False,
    )
```

```python
import functools
import jax
import jax.numpy as jnp
from jax import lax
from jax.experimental import pallas as pl
from jax.experimental.pallas import tpu as pltpu
from jax.sharding import PartitionSpec as P

F32 = jnp.float32
BF16 = jnp.bfloat16
LANES = 128
PHASE = 0.3
EPS = 1e-05
MIB = 1024 * 1024
RING = 4
WHOLE = pl.BlockSpec(memory_space=pltpu.VMEM)
SCALARS = pl.BlockSpec(memory_space=pltpu.SMEM)


def params(mib):
    return pltpu.CompilerParams(vmem_limit_bytes=mib * MIB)


def cost(flops, moved):
    return pl.CostEstimate(flops=flops, bytes_accessed=moved, transcendentals=0)


def split_kernel(slices, img_ref, out_ref, scratch):
    step, rows, _ = img_ref.shape
    block_rows = rows // slices
    for h in range(2):
        half = img_ref[:, :, h * LANES : (h + 1) * LANES].astype(F32)
        scratch[h] = half.reshape(step * rows, LANES)
    for j in range(slices):
        for b in range(block_rows):
            picked = pl.ds(j * block_rows + b, step, stride=rows)
            for h in range(2):
                out_ref[2 * b + h, j] = scratch[h, picked, :].astype(BF16)


def split_images(images, slices):
    particles, rows, width = images.shape
    block_rows = rows // slices
    step = 16
    return pl.pallas_call(
        functools.partial(split_kernel, slices),
        grid=(particles // step,),
        in_specs=[pl.BlockSpec((step, rows, width), lambda i: (i, 0, 0))],
        out_specs=pl.BlockSpec((2 * block_rows, slices, step, LANES), lambda i: (0, 0, i, 0)),
        out_shape=pltpu.HBM((2 * block_rows, slices, particles, LANES), BF16),
        scratch_shapes=[pltpu.VMEM((2, step * rows, LANES), F32)],
        compiler_params=params(56),
        cost_estimate=cost(0, images.size * 4),
    )(images)


def meta_kernel(
    capacity, blocks, owned, owner_ref, assign_ref, orient_ref, focus_ref, table_ref, meta_ref
):
    slices, particles = owner_ref.shape
    turns = table_ref.shape[1]
    count = slices * particles
    owners = (meta_ref.shape[2] - 2 * count - LANES) // capacity
    turn = lax.broadcasted_iota(jnp.int32, (turns, particles), 0)
    one_hot = (turn == orient_ref[...]).astype(BF16)
    place = jnp.dot(table_ref[...].astype(F32).astype(BF16), one_hot, preferred_element_type=F32)
    place = place + (assign_ref[...] * owned).astype(F32)
    owner = owner_ref[...].astype(F32)
    owner_row = jnp.concatenate([owner[j : j + 1, :] for j in range(slices)], axis=1)
    place_row = jnp.concatenate([place[j : j + 1, :] for j in range(slices)], axis=1)
    holder = lax.broadcasted_iota(jnp.int32, (owners, count), 0).astype(F32)
    match = (holder == owner_row).astype(BF16)
    before = lax.broadcasted_iota(jnp.int32, (count, count), 0)
    before = before < lax.broadcasted_iota(jnp.int32, (count, count), 1)
    earlier = jnp.dot(match, before.astype(BF16), preferred_element_type=F32)
    rank = jnp.sum(earlier * match.astype(F32), axis=0, keepdims=True)
    slot = owner_row * float(capacity) + rank
    slot_col = jnp.broadcast_to(slot, (8, count)).T[:, :1]
    every = lax.broadcasted_iota(jnp.int32, (count, owners * capacity), 1).astype(F32)
    at_slot = (every == slot_col).astype(BF16)
    shifted = jnp.broadcast_to(place_row + 1.0, (8, count)).astype(BF16)
    filled = jnp.dot(shifted, at_slot, preferred_element_type=F32)[:1] - 1.0
    last = 2 * count + owners * capacity
    tail = jnp.zeros((1, meta_ref.shape[2] - last - particles), F32)
    focus = jnp.concatenate([focus_ref[...].astype(F32), tail], axis=1)
    for d in range(meta_ref.shape[0]):
        meta_ref[d, :, :count] = owner_row * float(blocks) + place_row
        meta_ref[d, :, count : 2 * count] = slot
        meta_ref[d, :, 2 * count : last] = filled
        meta_ref[d, :, last:] = focus


def make_meta(owner, assign, orient, defocus, table, capacity, owners, blocks, owned, copies):
    particles, slices = owner.shape
    length = 2 * slices * particles + owners * capacity + LANES
    return pl.pallas_call(
        functools.partial(meta_kernel, capacity, blocks, owned),
        out_shape=jax.ShapeDtypeStruct((copies, 1, length), F32),
        compiler_params=params(56),
        cost_estimate=cost(100 * MIB, MIB),
    )(owner.T, assign[None, :], orient[None, :], defocus[None, :], table.T)


def after_kernel(x_ref, y_ref, z_ref, out_ref):
    pass


def after(x, y, z):
    hbm = pl.BlockSpec(memory_space=pltpu.HBM)
    anywhere = pl.BlockSpec(memory_space=pl.ANY)
    return pl.pallas_call(
        after_kernel,
        in_specs=[hbm, anywhere, anywhere],
        out_specs=hbm,
        out_shape=pltpu.HBM(x.shape, x.dtype),
        input_output_aliases={0: 0},
        compiler_params=params(1),
    )(x, y, z)


def contrast_kernel(extent, start, row_ref, meta_ref, ctf_ref):
    held, slices, particles, _ = ctf_ref.shape
    for k in range(held):
        focus = meta_ref[k, :, start : start + LANES]
        focus = jnp.broadcast_to(focus, (LANES, LANES)).T[:particles, :] / extent
        column = lax.broadcasted_iota(jnp.int32, (particles, LANES), 1).astype(F32)
        angle = focus * (column * column)
        cos_col, sin_col = jnp.cos(angle), jnp.sin(angle)
        row = column * 8.0 + row_ref[0]
        angle = focus * (row * row) + PHASE
        cos_row, sin_row = jnp.cos(angle), jnp.sin(angle)
        for j in range(slices):
            ctf_ref[k, j] = sin_row[:, j : j + 1] * cos_col + cos_row[:, j : j + 1] * sin_col


def contrast(row, meta, start, slices, particles, extent):
    senders, _, length = meta.shape
    held = 4
    return pl.pallas_call(
        functools.partial(contrast_kernel, extent, start),
        grid=(senders // held,),
        in_specs=[SCALARS, pl.BlockSpec((held, 1, length), lambda i: (i, 0, 0))],
        out_specs=pl.BlockSpec((held, slices, particles, LANES), lambda i: (i, 0, 0, 0)),
        out_shape=pltpu.HBM((senders, slices, particles, LANES), F32),
        compiler_params=params(8),
        cost_estimate=cost(1000 * MIB, 4 * MIB),
    )(row, meta)


def project_kernel(
    count, at_ref, meta_ref, ctf_ref, vol0, vol1, vol2, vol3, proj_ref, power_ref, pairs, one_hot
):
    taken, slices, particles, _ = proj_ref.shape
    held, blocks, _ = vol0.shape
    owned = blocks // 2
    holders = RING * held

    @pl.when(pl.program_id(0) == 0)
    def _():
        for t, vol in enumerate((vol0, vol1, vol2, vol3)):
            for i in range(held):
                where = pl.ds((t * held + i) * owned, owned)
                pairs[where, :LANES] = vol[i, :owned, :]
                pairs[where, LANES:] = vol[i, owned:, :]

    at_y = at_ref[0].astype(F32)
    at_z = at_ref[1].astype(F32)
    lane = lax.broadcasted_iota(jnp.int32, (count, LANES), 1).astype(F32)
    zero = jnp.zeros((count, owned), BF16)
    uppers = []
    for k in range(taken):
        key = meta_ref[k, :, :count]
        owner = jnp.floor(key * (1.0 / blocks))
        place = key - owner * float(blocks)
        upper = (place >= float(owned)).astype(F32)
        place = place - upper * float(owned)
        y = jnp.floor(owner * (1.0 / held))
        z = at_z - (owner - y * float(held))
        y = at_y - y
        y = jnp.where(y < 0.0, y + float(RING), y)
        z = jnp.where(z < 0.0, z + float(RING), z)
        rows = jnp.concatenate([place] * 8 + [upper] * 8 + [y * float(held) + z] * 8, axis=0).T
        hit = jnp.broadcast_to(rows[:, :1], (count, LANES)) == lane
        hit = hit.astype(BF16)
        uppers.append(jnp.broadcast_to(rows[:, 8:9], (count, LANES)) > 0.5)
        holder = jnp.broadcast_to(rows[:, 16:17], (count, LANES)).astype(BF16)
        for i in range(holders):
            one_hot[k, :, i * owned : (i + 1) * owned] = jnp.where(holder == i, hit, zero)
    powers = []
    for k in range(taken):
        acc = jnp.dot(one_hot[k], pairs[...], preferred_element_type=F32)
        picked = jnp.where(uppers[k], acc[:, LANES:], acc[:, :LANES])
        picked = picked.reshape(slices, particles, LANES)
        power = jnp.zeros((particles, LANES), F32)
        for j in range(slices):
            proj = ctf_ref[k, j] * picked[j]
            power += proj * proj
            proj_ref[k, j] = proj
        powers.append(power)
    power_ref[...] = jnp.sum(jnp.concatenate(powers, axis=0).T, axis=0, keepdims=True)


def project(at, meta, ctf, vols):
    senders, slices, particles, _ = ctf.shape
    held, blocks, _ = vols[0].shape
    span = RING * held * blocks // 2
    count = slices * particles
    taken = 4
    block = pl.BlockSpec((taken, slices, particles, LANES), lambda i: (i, 0, 0, 0))
    return pl.pallas_call(
        functools.partial(project_kernel, count),
        grid=(senders // taken,),
        in_specs=[
            SCALARS,
            pl.BlockSpec((taken, 1, meta.shape[2]), lambda i: (i, 0, 0)),
            block,
        ]
        + [pl.BlockSpec((held, blocks, LANES), lambda i: (0, 0, 0))] * RING,
        out_specs=[block, pl.BlockSpec((1, taken * particles), lambda i: (0, i))],
        out_shape=[
            pltpu.HBM(ctf.shape, F32),
            jax.ShapeDtypeStruct((1, senders * particles), F32),
        ],
        scratch_shapes=[
            pltpu.VMEM((span, 2 * LANES), BF16),
            pltpu.VMEM((taken, count, span), BF16),
        ],
        compiler_params=params(24),
        cost_estimate=cost(2 * senders * count * span * 2 * LANES, 10 * MIB),
    )(at, meta, ctf, *vols)


def sums_kernel(img_ref, proj_ref, power_ref, out_ref, cross, noise):
    senders, slices, particles, _ = img_ref.shape

    @pl.loop(0, senders)
    def _(s):
        cross_sum = jnp.zeros((particles, LANES), F32)
        noise_sum = jnp.zeros((particles, LANES), F32)
        for j in range(slices):
            img = img_ref[s, j].astype(F32)
            cross_sum += img * proj_ref[s, j]
            noise_sum += img * img
        cross[pl.ds(s * particles, particles), :] = cross_sum
        noise[pl.ds(s * particles, particles), :] = noise_sum

    total = senders * particles
    rows = [jnp.sum(ref[...].T, axis=0, keepdims=True) for ref in (cross, noise)]
    rows.append(power_ref[...])
    for d in range(senders):
        for i, row in enumerate(rows):
            out_ref[d, :, i * total : (i + 1) * total] = row


def partial_sums(img, proj, power):
    senders, slices, particles, _ = img.shape
    total = senders * particles
    return pl.pallas_call(
        sums_kernel,
        in_specs=[WHOLE] * 3,
        out_specs=WHOLE,
        out_shape=jax.ShapeDtypeStruct((senders, 1, 3 * total), F32),
        scratch_shapes=[pltpu.VMEM((total, LANES), F32)] * 2,
        compiler_params=params(12),
        cost_estimate=cost(img.size * 4, img.size * 6),
    )(img, proj, power)


def terms_kernel(pixels, part_ref, img_ref, ctf_ref, terms_ref, corr_ref, weight_col):
    senders, slices, particles, _ = img_ref.shape
    total = senders * particles
    sums = part_ref[0]
    for d in range(1, senders):
        sums = sums + part_ref[d]
    cross, power = sums[:, :total], sums[:, 2 * total :]
    noise = sums[:, total : 2 * total] / pixels + EPS
    corr = cross / jnp.sqrt((power + EPS) * noise)
    corr_ref[...] = corr
    weight = jax.nn.sigmoid(corr) / noise
    weight_col[...] = jnp.broadcast_to(weight, (LANES, total)).T

    @pl.loop(0, senders)
    def _(s):
        weight = weight_col[pl.ds(s * particles, particles), :]
        for j in range(slices):
            ctf = ctf_ref[s, j]
            scaled = weight * ctf
            rows = pl.ds(j * particles, particles)
            terms_ref[s, rows, :LANES] = (scaled * img_ref[s, j].astype(F32)).astype(BF16)
            terms_ref[s, rows, LANES:] = (scaled * ctf).astype(BF16)


def make_terms(partials, img, ctf, pixels):
    senders, slices, particles, _ = img.shape
    total = senders * particles
    return pl.pallas_call(
        functools.partial(terms_kernel, float(pixels)),
        in_specs=[WHOLE] * 3,
        out_specs=[WHOLE] * 2,
        out_shape=[
            jax.ShapeDtypeStruct((senders, slices * particles, 2 * LANES), BF16),
            jax.ShapeDtypeStruct((1, total), F32),
        ],
        scratch_shapes=[pltpu.VMEM((total, LANES), F32)],
        compiler_params=params(12),
        cost_estimate=cost(img.size * 4, img.size * 10),
    )(partials, img, ctf)


def scatter_kernel(capacity, offsets, at_ref, slot_ref, place_ref, terms_ref, out_ref, sorted_ref):
    senders, rows, width = terms_ref.shape
    blocks = out_ref.shape[1] * 2 // 3
    owned = blocks // 2
    holders = [at_ref[0] * RING + lax.rem(at_ref[1] + u, RING) for u in offsets]
    place_in = lax.broadcasted_iota(jnp.int32, (capacity, rows), 0)
    slot_at = [(place_in + h * capacity).astype(F32) for h in holders]
    slot_at = jnp.concatenate(slot_at, axis=0)
    for s in range(senders):
        pick = (slot_at == slot_ref[s]).astype(BF16)
        got = jnp.dot(pick, terms_ref[s], preferred_element_type=F32).astype(BF16)
        for i in range(len(offsets)):
            sorted_ref[i, s * capacity : (s + 1) * capacity, :] = got[
                i * capacity : (i + 1) * capacity
            ]
    block_at = lax.broadcasted_iota(jnp.int32, (blocks, senders * capacity), 0).astype(F32)
    for i, h in enumerate(holders):
        one_hot = (block_at == place_ref[h]).astype(BF16)
        summed = jnp.dot(one_hot, sorted_ref[i], preferred_element_type=F32)
        denom = jnp.where(at_ref[2] == 0, summed[:owned, LANES:], summed[owned:, LANES:])
        out_ref[i, :blocks, :] = summed[:, :LANES].astype(out_ref.dtype)
        out_ref[i, blocks:, :] = denom.astype(out_ref.dtype)


def scatter(at, offsets, slots, places, terms, blocks, capacity, kind):
    senders, rows, width = terms.shape
    held = len(offsets)
    return pl.pallas_call(
        functools.partial(scatter_kernel, capacity, offsets),
        in_specs=[SCALARS] + [WHOLE] * 3,
        out_specs=WHOLE,
        out_shape=jax.ShapeDtypeStruct((held, blocks * 3 // 2, LANES), kind),
        scratch_shapes=[pltpu.VMEM((held, senders * capacity, width), BF16)],
        compiler_params=params(12),
        cost_estimate=cost(
            2 * senders * held * capacity * width * (rows + blocks), 5 * MIB
        ),
    )(at, slots, places, terms)


def fold_kernel(own_ref, got1, got2, got3, *outs):
    for i, ref in enumerate(outs):
        total = own_ref[i]
        for got in (got1, got2, got3):
            total = total + got[i].astype(F32)
        ref[...] = total.astype(ref.dtype)


def fold(own, got, kinds):
    _, rows, width = own.shape
    return pl.pallas_call(
        fold_kernel,
        in_specs=[WHOLE] * 4,
        out_specs=[WHOLE] * len(kinds),
        out_shape=[jax.ShapeDtypeStruct((rows, width), k) for k in kinds],
        compiler_params=params(4),
        cost_estimate=cost(own.size * 4, own.size * 11),
    )(own, *got)


def ring(x, axis, size, step, shift):
    def target(i):
        place = i // step % RING
        return i + ((place + shift) % RING - place) * step

    return lax.ppermute(x, axis, [(i, target(i)) for i in range(size)])


def shards(images, defocus, assign, orient, owner, slice_loc, volume):
    owners = lax.axis_size("cls")
    groups = lax.axis_size("dom")
    me = lax.axis_index("dom")
    at = lax.axis_index("cls")
    at_y, at_z = at // RING, at % RING
    particles, image_rows, width = images.shape
    classes, owned, block_len = volume.shape
    slices = owner.shape[1]
    blocks = classes * owned
    rows = slices * particles
    capacity = 5 * rows // (2 * owners)

    at_yz = jnp.stack([at_y, at_z])

    meta = make_meta(
        owner, assign, orient, defocus, slice_loc, capacity, owners, blocks, owned, groups
    )
    meta = lax.all_to_all(meta, "dom", 0, 0, tiled=True)
    piece = lax.dynamic_slice_in_dim(volume, me * LANES, LANES, axis=2).reshape(blocks, LANES)
    near = jnp.stack([piece] + [ring(piece, "cls", owners, 1, t) for t in range(1, RING)])
    img = after(split_images(images, slices), near, meta)
    img = lax.all_to_all(img, "dom", 0, 0, tiled=True)
    vols = [near] + [ring(near, "cls", owners, RING, t) for t in range(1, RING)]

    slots = meta[:, :, rows : 2 * rows]
    last = 2 * rows + owners * capacity
    filled = meta[:, 0, 2 * rows : last].reshape(groups, owners, capacity).transpose(1, 0, 2)
    filled = filled.reshape(owners, 1, groups * capacity)

    row = (me // 2).astype(F32).reshape(1)
    ctf = contrast(row, meta, last, slices, particles, float(image_rows * image_rows))
    proj, power = project(at_yz, meta, ctf, vols)
    partial = partial_sums(img, proj, power)
    partial = lax.all_to_all(partial, "dom", 0, 0, tiled=True)
    terms, corr = make_terms(partial, img, ctf, image_rows * width)
    correlation = lax.dynamic_slice_in_dim(corr[0], me * particles, particles)

    def by_y(offsets, kinds):
        def part(t, kind):
            to = jnp.stack([(at_y + t) % RING, at_z, me % 2])
            return scatter(to, offsets, slots, filled, terms, blocks, capacity, kind)

        got = [ring(part(t, BF16), "cls", owners, RING, t) for t in (2, 1, 3)]
        return fold(part(0, F32), got, kinds)

    far, right = by_y((2, 1), (BF16, BF16))
    far, right = ring(far, "cls", owners, 1, 2), ring(right, "cls", owners, 1, 1)
    left, total = by_y((3, 0), (BF16, F32))
    left = ring(left, "cls", owners, 1, 3)
    total = total + far.astype(F32) + right.astype(F32) + left.astype(F32)
    numer, mine = total[:blocks], total[blocks:]
    other = lax.ppermute(mine, "dom", [(i, i ^ 1) for i in range(groups)])
    first = me % 2 == 0
    denom = jnp.concatenate([jnp.where(first, mine, other), jnp.where(first, other, mine)])
    new_volume = numer / (denom + 1.0)
    return (new_volume.reshape(classes, owned, LANES), correlation)


def solution(mesh):
    placed = (
        P(("dom", "cls"), None, None),
        P(("dom", "cls")),
        P(("dom", "cls")),
        P(("dom", "cls")),
        P(("dom", "cls"), None),
        P(),
        P(None, "cls", None),
    )
    return jax.shard_map(
        shards,
        mesh=mesh,
        in_specs=placed,
        out_specs=(P(None, "cls", "dom"), P(("dom", "cls"))),
        check_vma=False,
    )
```

```python
import functools
import jax
import jax.numpy as jnp
from jax import lax
from jax.experimental import pallas as pl
from jax.experimental.pallas import tpu as pltpu
from jax.sharding import PartitionSpec as P

F32 = jnp.float32
BF16 = jnp.bfloat16
LANES = 128
PHASE = 0.3
EPS = 1e-05
MIB = 1024 * 1024
RING = 4
PACK = 16
WHOLE = pl.BlockSpec(memory_space=pltpu.VMEM)
SCALARS = pl.BlockSpec(memory_space=pltpu.SMEM)


def params(mib):
    return pltpu.CompilerParams(vmem_limit_bytes=mib * MIB)


def cost(flops, moved):
    return pl.CostEstimate(flops=flops, bytes_accessed=moved, transcendentals=0)


def split_kernel(slices, img_ref, out_ref):
    particles, rows, _ = img_ref.shape
    block_rows = out_ref.shape[0] // 2
    together = PACK // block_rows
    size = PACK * PACK
    to = lax.broadcasted_iota(jnp.int32, (size, size), 0)
    come = lax.broadcasted_iota(jnp.int32, (size, size), 1)
    moved = (come == (to % PACK) * PACK + to // PACK).astype(BF16)
    for g in range(rows // PACK):
        for i in range(particles // PACK):
            part = img_ref[i * PACK : (i + 1) * PACK, g * PACK : (g + 1) * PACK, :]
            part = part.reshape(size, 2 * LANES)
            got = jnp.dot(moved, part, preferred_element_type=F32).astype(BF16)
            for k in range(PACK):
                j, b = g * together + k // block_rows, k % block_rows
                for h in range(2):
                    out_ref[2 * b + h, j, i * PACK : (i + 1) * PACK, :] = got[
                        k * PACK : (k + 1) * PACK, h * LANES : (h + 1) * LANES
                    ]


def split_images(images, slices):
    particles, rows, width = images.shape
    block_rows = rows // slices
    steps = 2
    return pl.pallas_call(
        functools.partial(split_kernel, slices),
        grid=(steps,),
        in_specs=[pl.BlockSpec((particles, rows // steps, width), lambda i: (0, i, 0))],
        out_specs=pl.BlockSpec(
            (2 * block_rows, slices // steps, particles, LANES), lambda i: (0, i, 0, 0)
        ),
        out_shape=pltpu.HBM((2 * block_rows, slices, particles, LANES), BF16),
        compiler_params=params(56),
        cost_estimate=cost(2 * images.size * PACK * PACK, images.size * 4),
    )(images)


def meta_kernel(
    capacity, blocks, owned, owner_ref, assign_ref, orient_ref, focus_ref, table_ref, meta_ref
):
    slices, particles = owner_ref.shape
    turns = table_ref.shape[1]
    count = slices * particles
    owners = (meta_ref.shape[2] - 2 * count - LANES) // capacity
    turn = lax.broadcasted_iota(jnp.int32, (turns, particles), 0)
    one_hot = (turn == orient_ref[...]).astype(BF16)
    place = jnp.dot(table_ref[...].astype(F32).astype(BF16), one_hot, preferred_element_type=F32)
    place = place + (assign_ref[...] * owned).astype(F32)
    owner = owner_ref[...].astype(F32)
    owner_row = jnp.concatenate([owner[j : j + 1, :] for j in range(slices)], axis=1)
    place_row = jnp.concatenate([place[j : j + 1, :] for j in range(slices)], axis=1)
    holder = lax.broadcasted_iota(jnp.int32, (owners, count), 0).astype(F32)
    match = (holder == owner_row).astype(BF16)
    before = lax.broadcasted_iota(jnp.int32, (count, count), 0)
    before = before < lax.broadcasted_iota(jnp.int32, (count, count), 1)
    earlier = jnp.dot(match, before.astype(BF16), preferred_element_type=F32)
    rank = jnp.sum(earlier * match.astype(F32), axis=0, keepdims=True)
    slot = owner_row * float(capacity) + rank
    slot_col = jnp.broadcast_to(slot, (8, count)).T[:, :1]
    every = lax.broadcasted_iota(jnp.int32, (count, owners * capacity), 1).astype(F32)
    at_slot = (every == slot_col).astype(BF16)
    shifted = jnp.broadcast_to(place_row + 1.0, (8, count)).astype(BF16)
    filled = jnp.dot(shifted, at_slot, preferred_element_type=F32)[:1] - 1.0
    last = 2 * count + owners * capacity
    tail = jnp.zeros((1, meta_ref.shape[2] - last - particles), F32)
    focus = jnp.concatenate([focus_ref[...].astype(F32), tail], axis=1)
    for d in range(meta_ref.shape[0]):
        meta_ref[d, :, :count] = owner_row * float(blocks) + place_row
        meta_ref[d, :, count : 2 * count] = slot
        meta_ref[d, :, 2 * count : last] = filled
        meta_ref[d, :, last:] = focus


def make_meta(owner, assign, orient, defocus, table, capacity, owners, blocks, owned, copies):
    particles, slices = owner.shape
    length = 2 * slices * particles + owners * capacity + LANES
    return pl.pallas_call(
        functools.partial(meta_kernel, capacity, blocks, owned),
        out_shape=jax.ShapeDtypeStruct((copies, 1, length), F32),
        compiler_params=params(56),
        cost_estimate=cost(100 * MIB, MIB),
    )(owner.T, assign[None, :], orient[None, :], defocus[None, :], table.T)


def after_kernel(x_ref, y_ref, z_ref, out_ref):
    pass


def after(x, y, z):
    hbm = pl.BlockSpec(memory_space=pltpu.HBM)
    anywhere = pl.BlockSpec(memory_space=pl.ANY)
    return pl.pallas_call(
        after_kernel,
        in_specs=[hbm, anywhere, anywhere],
        out_specs=hbm,
        out_shape=pltpu.HBM(x.shape, x.dtype),
        input_output_aliases={0: 0},
        compiler_params=params(1),
    )(x, y, z)


def contrast_kernel(extent, capacity, at_ref, meta_ref, ctf_ref, place_ref):
    held, slices, particles, _ = ctf_ref.shape
    owners = place_ref.shape[0]
    start = meta_ref.shape[2] - LANES
    for k in range(held):
        focus = meta_ref[k, :, start:]
        focus = jnp.broadcast_to(focus, (LANES, LANES)).T[:particles, :] / extent
        column = lax.broadcasted_iota(jnp.int32, (particles, LANES), 1).astype(F32)
        angle = focus * (column * column)
        cos_col, sin_col = jnp.cos(angle), jnp.sin(angle)
        row = column * 8.0 + at_ref[3].astype(F32)
        angle = focus * (row * row) + PHASE
        cos_row, sin_row = jnp.cos(angle), jnp.sin(angle)
        for j in range(slices):
            ctf_ref[k, j] = sin_row[:, j : j + 1] * cos_col + cos_row[:, j : j + 1] * sin_col

    first = start - owners * capacity
    for i in range(place_ref.shape[2] // (held * capacity)):

        @pl.when(pl.program_id(0) == i)
        def _():
            for h in range(owners):
                at = first + h * capacity
                got = [meta_ref[k, :, at : at + capacity] for k in range(held)]
                to = i * held * capacity
                place_ref[h, :, to : to + held * capacity] = jnp.concatenate(got, axis=1)


def contrast(at, meta, slices, particles, owners, capacity, extent):
    senders, _, length = meta.shape
    held = 4
    return pl.pallas_call(
        functools.partial(contrast_kernel, extent, capacity),
        grid=(senders // held,),
        in_specs=[SCALARS, pl.BlockSpec((held, 1, length), lambda i: (i, 0, 0))],
        out_specs=[
            pl.BlockSpec((held, slices, particles, LANES), lambda i: (i, 0, 0, 0)),
            pl.BlockSpec((owners, 1, senders * capacity), lambda i: (0, 0, 0)),
        ],
        out_shape=[
            pltpu.HBM((senders, slices, particles, LANES), F32),
            jax.ShapeDtypeStruct((owners, 1, senders * capacity), F32),
        ],
        compiler_params=params(32),
        cost_estimate=cost(MIB, MIB),
    )(at, meta)


def project_kernel(
    count, at_ref, meta_ref, ctf_ref, vol0, vol1, vol2, vol3, proj_ref, power_ref, pairs
):
    taken, slices, particles, _ = proj_ref.shape
    held, blocks, _ = vol0.shape
    owned = blocks // 2
    holders = RING * held

    @pl.when(pl.program_id(0) == 0)
    def _():
        for t, vol in enumerate((vol0, vol1, vol2, vol3)):
            for i in range(held):
                where = pl.ds((t * held + i) * owned, owned)
                pairs[where, :LANES] = vol[i, :owned, :]
                pairs[where, LANES:] = vol[i, owned:, :]

    at_y = at_ref[0].astype(F32)
    at_z = at_ref[1].astype(F32)
    lane = lax.broadcasted_iota(jnp.int32, (count, LANES), 1).astype(F32)
    zero = jnp.zeros((count, owned), BF16)
    powers = []
    for k in range(taken):
        key = meta_ref[k, :, :count]
        owner = jnp.floor(key * (1.0 / blocks))
        place = key - owner * float(blocks)
        upper = (place >= float(owned)).astype(F32)
        place = place - upper * float(owned)
        y = jnp.floor(owner * (1.0 / held))
        z = at_z - (owner - y * float(held))
        y = at_y - y
        y = jnp.where(y < 0.0, y + float(RING), y)
        z = jnp.where(z < 0.0, z + float(RING), z)
        rows = jnp.concatenate([place] * 8 + [upper] * 8 + [y * float(held) + z] * 8, axis=0).T
        hit = jnp.broadcast_to(rows[:, :1], (count, LANES)) == lane
        hit = hit.astype(BF16)
        upper = jnp.broadcast_to(rows[:, 8:9], (count, LANES)) > 0.5
        holder = jnp.broadcast_to(rows[:, 16:17], (count, LANES)).astype(BF16)
        acc = jnp.zeros((count, 2 * LANES), F32)
        for i in range(0, holders, held):
            one_hot = [jnp.where(holder == i + q, hit, zero) for q in range(held)]
            one_hot = jnp.concatenate(one_hot, axis=1)
            some = pairs[i * owned : (i + held) * owned, :]
            acc += jnp.dot(one_hot, some, preferred_element_type=F32)
        picked = jnp.where(upper, acc[:, LANES:], acc[:, :LANES])
        picked = picked.reshape(slices, particles, LANES)
        power = jnp.zeros((particles, LANES), F32)
        for j in range(slices):
            proj = ctf_ref[k, j] * picked[j]
            power += proj * proj
            proj_ref[k, j] = proj
        powers.append(power)
    power_ref[...] = jnp.sum(jnp.concatenate(powers, axis=0).T, axis=0, keepdims=True)


def project(at, meta, ctf, vols):
    senders, slices, particles, _ = ctf.shape
    held, blocks, _ = vols[0].shape
    span = RING * held * blocks // 2
    count = slices * particles
    taken = 8
    block = pl.BlockSpec((taken, slices, particles, LANES), lambda i: (i, 0, 0, 0))
    return pl.pallas_call(
        functools.partial(project_kernel, count),
        grid=(senders // taken,),
        in_specs=[
            SCALARS,
            pl.BlockSpec((taken, 1, meta.shape[2]), lambda i: (i, 0, 0)),
            block,
        ]
        + [pl.BlockSpec((held, blocks, LANES), lambda i: (0, 0, 0))] * RING,
        out_specs=[block, pl.BlockSpec((1, taken * particles), lambda i: (0, i))],
        out_shape=[
            pltpu.HBM(ctf.shape, F32),
            jax.ShapeDtypeStruct((1, senders * particles), F32),
        ],
        scratch_shapes=[pltpu.VMEM((span, 2 * LANES), BF16)],
        compiler_params=params(32),
        cost_estimate=cost(5 * 2 * senders * count * span * 2 * LANES, 10 * MIB),
    )(at, meta, in_hbm(ctf), *vols)


def in_hbm(x):
    return pltpu.with_memory_space_constraint(x, pltpu.HBM)


def fetch(src, dst, sems):
    parts = sems.shape[0]
    size = src.shape[0] // parts
    copies = []
    for i in range(parts):
        at = pl.ds(i * size, size)
        copies.append(pltpu.make_async_copy(src.at[at], dst.at[at], sems.at[i]))
        copies[-1].start()
    return copies


def sums_kernel(img_ref, proj_hbm, power_hbm, out_ref, cross, noise, power, proj, sems, sem):
    senders, slices, particles, _ = img_ref.shape
    copies = fetch(proj_hbm, proj, sems)
    last = pltpu.make_async_copy(power_hbm, power, sem)
    last.start()
    size = senders // len(copies)
    for i, copy in enumerate(copies):
        copy.wait()

        @pl.loop(i * size, (i + 1) * size)
        def _(s):
            cross_sum = jnp.zeros((particles, LANES), F32)
            noise_sum = jnp.zeros((particles, LANES), F32)
            for j in range(slices):
                img = img_ref[s, j].astype(F32)
                cross_sum += img * proj[s, j]
                noise_sum += img * img
            cross[pl.ds(s * particles, particles), :] = cross_sum
            noise[pl.ds(s * particles, particles), :] = noise_sum

    total = senders * particles
    rows = [jnp.sum(ref[...].T, axis=0, keepdims=True) for ref in (cross, noise)]
    last.wait()
    rows.append(power[...])
    for d in range(senders):
        for i, row in enumerate(rows):
            out_ref[d, :, i * total : (i + 1) * total] = row


def partial_sums(img, proj, power):
    senders, slices, particles, _ = img.shape
    total = senders * particles
    return pl.pallas_call(
        sums_kernel,
        in_specs=[WHOLE] + [pl.BlockSpec(memory_space=pltpu.HBM)] * 2,
        out_specs=WHOLE,
        out_shape=jax.ShapeDtypeStruct((senders, 1, 3 * total), F32),
        scratch_shapes=[pltpu.VMEM((total, LANES), F32)] * 2
        + [
            pltpu.VMEM(power.shape, F32),
            pltpu.VMEM(proj.shape, F32),
            pltpu.SemaphoreType.DMA((4,)),
            pltpu.SemaphoreType.DMA,
        ],
        compiler_params=params(12),
        cost_estimate=cost(img.size * 4, img.size * 6),
    )(img, in_hbm(proj), in_hbm(power))


def terms_kernel(pixels, part_ref, img_ref, ctf_hbm, terms_ref, corr_ref, weight_col, ctf_all, sems):
    senders, slices, particles, _ = img_ref.shape
    total = senders * particles
    copies = fetch(ctf_hbm, ctf_all, sems)
    size = senders // len(copies)
    sums = part_ref[0]
    for d in range(1, senders):
        sums = sums + part_ref[d]
    cross, power = sums[:, :total], sums[:, 2 * total :]
    noise = sums[:, total : 2 * total] / pixels + EPS
    corr = cross / jnp.sqrt((power + EPS) * noise)
    corr_ref[...] = corr
    weight = jax.nn.sigmoid(corr) / noise
    weight_col[...] = jnp.broadcast_to(weight, (LANES, total)).T
    for i, copy in enumerate(copies):
        copy.wait()

        @pl.loop(i * size, (i + 1) * size)
        def _(s):
            weight = weight_col[pl.ds(s * particles, particles), :]
            for j in range(slices):
                ctf = ctf_all[s, j]
                scaled = weight * ctf
                rows = pl.ds(j * particles, particles)
                terms_ref[s, rows, :LANES] = (scaled * img_ref[s, j].astype(F32)).astype(BF16)
                terms_ref[s, rows, LANES:] = (scaled * ctf).astype(BF16)


def make_terms(partials, img, ctf, pixels):
    senders, slices, particles, _ = img.shape
    total = senders * particles
    return pl.pallas_call(
        functools.partial(terms_kernel, float(pixels)),
        in_specs=[WHOLE, WHOLE, pl.BlockSpec(memory_space=pltpu.HBM)],
        out_specs=[WHOLE] * 2,
        out_shape=[
            jax.ShapeDtypeStruct((senders, slices * particles, 2 * LANES), BF16),
            jax.ShapeDtypeStruct((1, total), F32),
        ],
        scratch_shapes=[
            pltpu.VMEM((total, LANES), F32),
            pltpu.VMEM(ctf.shape, F32),
            pltpu.SemaphoreType.DMA((4,)),
        ],
        compiler_params=params(12),
        cost_estimate=cost(img.size * 4, img.size * 10),
    )(partials, img, in_hbm(ctf))


def scatter_kernel(
    capacity, shift, offsets, at_ref, meta_ref, place_ref, terms_ref, out_ref, sorted_ref
):
    senders, rows, width = terms_ref.shape
    blocks = out_ref.shape[1] * 2 // 3
    owned = blocks // 2
    y = lax.rem(at_ref[0] + shift, RING)
    holders = [y * RING + lax.rem(at_ref[1] + u, RING) for u in offsets]
    place_in = lax.broadcasted_iota(jnp.int32, (capacity, rows), 0)
    slot_at = [(place_in + h * capacity).astype(F32) for h in holders]
    slot_at = jnp.concatenate(slot_at, axis=0)
    for s in range(senders):
        pick = (slot_at == meta_ref[s, :, rows : 2 * rows]).astype(BF16)
        got = jnp.dot(pick, terms_ref[s], preferred_element_type=F32).astype(BF16)
        for i in range(len(offsets)):
            sorted_ref[i, s * capacity : (s + 1) * capacity, :] = got[
                i * capacity : (i + 1) * capacity
            ]
    block_at = lax.broadcasted_iota(jnp.int32, (blocks, senders * capacity), 0).astype(F32)
    for i, h in enumerate(holders):
        one_hot = (block_at == place_ref[h]).astype(BF16)
        summed = jnp.dot(one_hot, sorted_ref[i], preferred_element_type=F32)
        denom = jnp.where(at_ref[2] == 0, summed[:owned, LANES:], summed[owned:, LANES:])
        out_ref[i, :blocks, :] = summed[:, :LANES].astype(out_ref.dtype)
        out_ref[i, blocks:, :] = denom.astype(out_ref.dtype)


def scatter(at, shift, offsets, meta, places, terms, blocks, capacity, kind):
    senders, rows, width = terms.shape
    held = len(offsets)
    out = jax.ShapeDtypeStruct((held, blocks * 3 // 2, LANES), kind)
    return pl.pallas_call(
        functools.partial(scatter_kernel, capacity, shift, offsets),
        in_specs=[SCALARS] + [WHOLE] * 3,
        out_specs=WHOLE,
        out_shape=out,
        scratch_shapes=[pltpu.VMEM((held, senders * capacity, width), BF16)],
        compiler_params=params(12),
        cost_estimate=cost(
            2 * senders * held * capacity * width * (rows + blocks), 5 * MIB
        ),
    )(at, meta, places, terms)


def fold_kernel(own_ref, got1, got2, got3, *outs):
    for i, ref in enumerate(outs):
        total = own_ref[i]
        for got in (got1, got2, got3):
            total = total + got[i].astype(F32)
        ref[...] = total.astype(ref.dtype)


def fold(own, got, kinds):
    _, rows, width = own.shape
    return pl.pallas_call(
        fold_kernel,
        in_specs=[WHOLE] * 4,
        out_specs=[WHOLE] * len(kinds),
        out_shape=[jax.ShapeDtypeStruct((rows, width), k) for k in kinds],
        compiler_params=params(4),
        cost_estimate=cost(own.size * 4, own.size * 11),
    )(own, *got)


def ring(x, axis, size, step, shift):
    def target(i):
        place = i // step % RING
        return i + ((place + shift) % RING - place) * step

    return lax.ppermute(x, axis, [(i, target(i)) for i in range(size)])


def shards(images, defocus, assign, orient, owner, slice_loc, volume):
    owners = lax.axis_size("cls")
    groups = lax.axis_size("dom")
    me = lax.axis_index("dom")
    at = lax.axis_index("cls")
    at_y, at_z = at // RING, at % RING
    particles, image_rows, width = images.shape
    classes, owned, block_len = volume.shape
    slices = owner.shape[1]
    blocks = classes * owned
    rows = slices * particles
    capacity = 5 * rows // (2 * owners)

    at_all = jnp.stack([at_y, at_z, me % 2, me // 2])

    meta = make_meta(
        owner, assign, orient, defocus, slice_loc, capacity, owners, blocks, owned, groups
    )
    meta = lax.all_to_all(meta, "dom", 0, 0, tiled=True)
    piece = lax.dynamic_slice_in_dim(volume, me * LANES, LANES, axis=2).reshape(blocks, LANES)
    near = jnp.stack([piece] + [ring(piece, "cls", owners, 1, t) for t in range(1, RING)])
    img = after(split_images(images, slices), near, meta)
    img = lax.all_to_all(img, "dom", 0, 0, tiled=True)
    vols = [near] + [ring(near, "cls", owners, RING, t) for t in range(1, RING)]

    extent = float(image_rows * image_rows)
    ctf, places = contrast(at_all, meta, slices, particles, owners, capacity, extent)
    proj, power = project(at_all, meta, ctf, vols)
    partial = partial_sums(img, proj, power)
    partial = lax.all_to_all(partial, "dom", 0, 0, tiled=True)
    terms, corr = make_terms(partial, img, ctf, image_rows * width)
    correlation = lax.dynamic_slice_in_dim(corr[0], me * particles, particles)

    parts = {}
    for t in (2, 1, 3, 0):
        kind = BF16 if t else F32
        parts[t] = scatter(at_all, t, (2, 1, 3, 0), meta, places, terms, blocks, capacity, kind)
    got = [ring(parts[t], "cls", owners, RING, t) for t in (2, 1, 3)]
    far, right, left, total = fold(parts[0], got, (BF16, BF16, BF16, F32))
    far = ring(far, "cls", owners, 1, 2)
    right = ring(right, "cls", owners, 1, 1)
    left = ring(left, "cls", owners, 1, 3)
    total = total + far.astype(F32) + right.astype(F32) + left.astype(F32)
    numer, mine = total[:blocks], total[blocks:]
    other = lax.ppermute(mine, "dom", [(i, i ^ 1) for i in range(groups)])
    first = me % 2 == 0
    denom = jnp.concatenate([jnp.where(first, mine, other), jnp.where(first, other, mine)])
    new_volume = numer / (denom + 1.0)
    return (new_volume.reshape(classes, owned, LANES), correlation)


def solution(mesh):
    placed = (
        P(("dom", "cls"), None, None),
        P(("dom", "cls")),
        P(("dom", "cls")),
        P(("dom", "cls")),
        P(("dom", "cls"), None),
        P(),
        P(None, "cls", None),
    )
    return jax.shard_map(
        shards,
        mesh=mesh,
        in_specs=placed,
        out_specs=(P(None, "cls", "dom"), P(("dom", "cls"))),
        check_vma=False,
    )
```

```python
import functools
import jax
import jax.numpy as jnp
from jax import lax
from jax.experimental import pallas as pl
from jax.experimental.pallas import tpu as pltpu
from jax.sharding import PartitionSpec as P

F32 = jnp.float32
BF16 = jnp.bfloat16
LANES = 128
PHASE = 0.3
EPS = 1e-05
MIB = 1024 * 1024
RING = 4
PACK = 16
WHOLE = pl.BlockSpec(memory_space=pltpu.VMEM)
SCALARS = pl.BlockSpec(memory_space=pltpu.SMEM)


def params(mib):
    return pltpu.CompilerParams(vmem_limit_bytes=mib * MIB)


def cost(flops, moved):
    return pl.CostEstimate(flops=flops, bytes_accessed=moved, transcendentals=0)


def in_vmem(x):
    return pltpu.with_memory_space_constraint(x, pltpu.VMEM)


def in_hbm(x):
    return pltpu.with_memory_space_constraint(x, pltpu.HBM)


def piece_kernel(column_ref, vol_hbm, out_ref, sem):
    at = pl.ds(pl.multiple_of(column_ref[0] * LANES, LANES), LANES)
    copy = pltpu.make_async_copy(vol_hbm.at[:, :, at], out_ref, sem)
    copy.start()
    copy.wait()


def piece_of(volume, column):
    classes, owned, _ = volume.shape
    return pl.pallas_call(
        piece_kernel,
        in_specs=[SCALARS, pl.BlockSpec(memory_space=pltpu.HBM)],
        out_specs=WHOLE,
        out_shape=jax.ShapeDtypeStruct((classes, owned, LANES), BF16),
        scratch_shapes=[pltpu.SemaphoreType.DMA],
        compiler_params=params(1),
        cost_estimate=cost(0, 4 * classes * owned * LANES),
    )(column.reshape(1), in_hbm(volume))


def split_kernel(slices, img_ref, out_ref):
    particles, rows, _ = img_ref.shape
    block_rows = out_ref.shape[0] // 2
    together = PACK // block_rows
    size = PACK * PACK
    to = lax.broadcasted_iota(jnp.int32, (size, size), 0)
    come = lax.broadcasted_iota(jnp.int32, (size, size), 1)
    moved = (come == (to % PACK) * PACK + to // PACK).astype(BF16)
    for g in range(rows // PACK):
        for i in range(particles // PACK):
            part = img_ref[i * PACK : (i + 1) * PACK, g * PACK : (g + 1) * PACK, :]
            part = part.reshape(size, 2 * LANES)
            got = jnp.dot(moved, part, preferred_element_type=F32).astype(BF16)
            for k in range(PACK):
                j, b = g * together + k // block_rows, k % block_rows
                for h in range(2):
                    out_ref[2 * b + h, j, i * PACK : (i + 1) * PACK, :] = got[
                        k * PACK : (k + 1) * PACK, h * LANES : (h + 1) * LANES
                    ]


def split_images(images, slices):
    particles, rows, width = images.shape
    block_rows = rows // slices
    steps = 2
    return pl.pallas_call(
        functools.partial(split_kernel, slices),
        grid=(steps,),
        in_specs=[pl.BlockSpec((particles, rows // steps, width), lambda i: (0, i, 0))],
        out_specs=pl.BlockSpec(
            (2 * block_rows, slices // steps, particles, LANES), lambda i: (0, i, 0, 0)
        ),
        out_shape=pltpu.HBM((2 * block_rows, slices, particles, LANES), BF16),
        compiler_params=params(56),
        cost_estimate=cost(2 * images.size * PACK * PACK, images.size * 4),
    )(images)


def meta_kernel(
    capacity, blocks, owned, owner_ref, assign_ref, orient_ref, focus_ref, table_ref, meta_ref
):
    slices, particles = owner_ref.shape
    turns = table_ref.shape[1]
    count = slices * particles
    owners = (meta_ref.shape[2] - 2 * count - LANES) // capacity
    turn = lax.broadcasted_iota(jnp.int32, (turns, particles), 0)
    one_hot = (turn == orient_ref[...]).astype(BF16)
    place = jnp.dot(table_ref[...].astype(F32).astype(BF16), one_hot, preferred_element_type=F32)
    place = place + (assign_ref[...] * owned).astype(F32)
    owner = owner_ref[...].astype(F32)
    owner_row = jnp.concatenate([owner[j : j + 1, :] for j in range(slices)], axis=1)
    place_row = jnp.concatenate([place[j : j + 1, :] for j in range(slices)], axis=1)
    holder = lax.broadcasted_iota(jnp.int32, (owners, count), 0).astype(F32)
    match = (holder == owner_row).astype(BF16)
    before = lax.broadcasted_iota(jnp.int32, (count, count), 0)
    before = before < lax.broadcasted_iota(jnp.int32, (count, count), 1)
    earlier = jnp.dot(match, before.astype(BF16), preferred_element_type=F32)
    rank = jnp.sum(earlier * match.astype(F32), axis=0, keepdims=True)
    slot = owner_row * float(capacity) + rank
    slot_col = jnp.broadcast_to(slot, (8, count)).T[:, :1]
    every = lax.broadcasted_iota(jnp.int32, (count, owners * capacity), 1).astype(F32)
    at_slot = (every == slot_col).astype(BF16)
    shifted = jnp.broadcast_to(place_row + 1.0, (8, count)).astype(BF16)
    filled = jnp.dot(shifted, at_slot, preferred_element_type=F32)[:1] - 1.0
    last = 2 * count + owners * capacity
    tail = jnp.zeros((1, meta_ref.shape[2] - last - particles), F32)
    focus = jnp.concatenate([focus_ref[...].astype(F32), tail], axis=1)
    for d in range(meta_ref.shape[0]):
        meta_ref[d, :, :count] = owner_row * float(blocks) + place_row
        meta_ref[d, :, count : 2 * count] = slot
        meta_ref[d, :, 2 * count : last] = filled
        meta_ref[d, :, last:] = focus


def make_meta(owner, assign, orient, defocus, table, capacity, owners, blocks, owned, copies):
    particles, slices = owner.shape
    length = 2 * slices * particles + owners * capacity + LANES
    return pl.pallas_call(
        functools.partial(meta_kernel, capacity, blocks, owned),
        out_shape=jax.ShapeDtypeStruct((copies, 1, length), F32),
        compiler_params=params(56),
        cost_estimate=cost(100 * MIB, MIB),
    )(owner.T, assign[None, :], orient[None, :], defocus[None, :], table.T)


def after_kernel(x_ref, y_ref, z_ref, out_ref):
    pass


def after(x, y, z):
    hbm = pl.BlockSpec(memory_space=pltpu.HBM)
    anywhere = pl.BlockSpec(memory_space=pl.ANY)
    return pl.pallas_call(
        after_kernel,
        in_specs=[hbm, anywhere, anywhere],
        out_specs=hbm,
        out_shape=pltpu.HBM(x.shape, x.dtype),
        input_output_aliases={0: 0},
        compiler_params=params(1),
    )(x, y, z)


def contrast_kernel(extent, capacity, at_ref, meta_ref, ctf_ref, place_ref):
    held, slices, particles, _ = ctf_ref.shape
    owners = place_ref.shape[0]
    start = meta_ref.shape[2] - LANES
    for k in range(held):
        focus = meta_ref[k, :, start:]
        focus = jnp.broadcast_to(focus, (LANES, LANES)).T[:particles, :] / extent
        column = lax.broadcasted_iota(jnp.int32, (particles, LANES), 1).astype(F32)
        angle = focus * (column * column)
        cos_col, sin_col = jnp.cos(angle), jnp.sin(angle)
        row = column * 8.0 + at_ref[3].astype(F32)
        angle = focus * (row * row) + PHASE
        cos_row, sin_row = jnp.cos(angle), jnp.sin(angle)
        for j in range(slices):
            ctf_ref[k, j] = sin_row[:, j : j + 1] * cos_col + cos_row[:, j : j + 1] * sin_col

    first = start - owners * capacity
    for i in range(place_ref.shape[2] // (held * capacity)):

        @pl.when(pl.program_id(0) == i)
        def _():
            for h in range(owners):
                at = first + h * capacity
                got = [meta_ref[k, :, at : at + capacity] for k in range(held)]
                to = i * held * capacity
                place_ref[h, :, to : to + held * capacity] = jnp.concatenate(got, axis=1)


def contrast(at, meta, slices, particles, owners, capacity, extent):
    senders, _, length = meta.shape
    held = 4
    return pl.pallas_call(
        functools.partial(contrast_kernel, extent, capacity),
        grid=(senders // held,),
        in_specs=[SCALARS, pl.BlockSpec((held, 1, length), lambda i: (i, 0, 0))],
        out_specs=[
            pl.BlockSpec((held, slices, particles, LANES), lambda i: (i, 0, 0, 0)),
            pl.BlockSpec((owners, 1, senders * capacity), lambda i: (0, 0, 0)),
        ],
        out_shape=[
            pltpu.VMEM((senders, slices, particles, LANES), F32),
            jax.ShapeDtypeStruct((owners, 1, senders * capacity), F32),
        ],
        compiler_params=params(12),
        cost_estimate=cost(MIB, MIB),
    )(at, meta)


def project_kernel(
    count, at_ref, meta_ref, ctf_ref, vol0, vol1, vol2, vol3, proj_ref, power_ref, pairs
):
    taken, slices, particles, _ = proj_ref.shape
    held, blocks, _ = vol0.shape
    owned = blocks // 2
    holders = RING * held

    @pl.when(pl.program_id(0) == 0)
    def _():
        for t, vol in enumerate((vol0, vol1, vol2, vol3)):
            for i in range(held):
                where = pl.ds((t * held + i) * owned, owned)
                pairs[where, :LANES] = vol[i, :owned, :]
                pairs[where, LANES:] = vol[i, owned:, :]

    at_y = at_ref[0].astype(F32)
    at_z = at_ref[1].astype(F32)
    lane = lax.broadcasted_iota(jnp.int32, (count, LANES), 1).astype(F32)
    zero = jnp.zeros((count, owned), BF16)
    powers = []
    for k in range(taken):
        key = meta_ref[k, :, :count]
        owner = jnp.floor(key * (1.0 / blocks))
        place = key - owner * float(blocks)
        upper = (place >= float(owned)).astype(F32)
        place = place - upper * float(owned)
        y = jnp.floor(owner * (1.0 / held))
        z = at_z - (owner - y * float(held))
        y = at_y - y
        y = jnp.where(y < 0.0, y + float(RING), y)
        z = jnp.where(z < 0.0, z + float(RING), z)
        rows = jnp.concatenate([place] * 8 + [upper] * 8 + [y * float(held) + z] * 8, axis=0).T
        hit = jnp.broadcast_to(rows[:, :1], (count, LANES)) == lane
        hit = hit.astype(BF16)
        upper = jnp.broadcast_to(rows[:, 8:9], (count, LANES)) > 0.5
        holder = jnp.broadcast_to(rows[:, 16:17], (count, LANES)).astype(BF16)
        acc = jnp.zeros((count, 2 * LANES), F32)
        for i in range(0, holders, held):
            one_hot = [jnp.where(holder == i + q, hit, zero) for q in range(held)]
            one_hot = jnp.concatenate(one_hot, axis=1)
            some = pairs[i * owned : (i + held) * owned, :]
            acc += jnp.dot(one_hot, some, preferred_element_type=F32)
        picked = jnp.where(upper, acc[:, LANES:], acc[:, :LANES])
        picked = picked.reshape(slices, particles, LANES)
        power = jnp.zeros((particles, LANES), F32)
        for j in range(slices):
            proj = ctf_ref[k, j] * picked[j]
            power += proj * proj
            proj_ref[k, j] = proj
        powers.append(power)
    power_ref[...] = jnp.sum(jnp.concatenate(powers, axis=0).T, axis=0, keepdims=True)


def project(at, meta, ctf, vols):
    senders, slices, particles, _ = ctf.shape
    held, blocks, _ = vols[0].shape
    span = RING * held * blocks // 2
    count = slices * particles
    taken = 4
    block = pl.BlockSpec((taken, slices, particles, LANES), lambda i: (i, 0, 0, 0))
    return pl.pallas_call(
        functools.partial(project_kernel, count),
        grid=(senders // taken,),
        in_specs=[
            SCALARS,
            pl.BlockSpec((taken, 1, meta.shape[2]), lambda i: (i, 0, 0)),
            block,
        ]
        + [pl.BlockSpec((held, blocks, LANES), lambda i: (0, 0, 0))] * RING,
        out_specs=[block, pl.BlockSpec((1, taken * particles), lambda i: (0, i))],
        out_shape=[
            pltpu.HBM(ctf.shape, F32),
            jax.ShapeDtypeStruct((1, senders * particles), F32),
        ],
        scratch_shapes=[pltpu.VMEM((span, 2 * LANES), BF16)],
        compiler_params=params(20),
        cost_estimate=cost(5 * 2 * senders * count * span * 2 * LANES, 10 * MIB),
    )(at, meta, in_vmem(ctf), *vols)


def fetch(src, dst, sems):
    parts = sems.shape[0]
    size = src.shape[0] // parts
    copies = []
    for i in range(parts):
        at = pl.ds(i * size, size)
        copies.append(pltpu.make_async_copy(src.at[at], dst.at[at], sems.at[i]))
        copies[-1].start()
    return copies


def sums_kernel(img_ref, proj_hbm, power_hbm, out_ref, cross, noise, power, proj, sems, sem):
    senders, slices, particles, _ = img_ref.shape
    copies = fetch(proj_hbm, proj, sems)
    last = pltpu.make_async_copy(power_hbm, power, sem)
    last.start()
    size = senders // len(copies)
    for i, copy in enumerate(copies):
        copy.wait()

        @pl.loop(i * size, (i + 1) * size)
        def _(s):
            cross_sum = jnp.zeros((particles, LANES), F32)
            noise_sum = jnp.zeros((particles, LANES), F32)
            for j in range(slices):
                img = img_ref[s, j].astype(F32)
                cross_sum += img * proj[s, j]
                noise_sum += img * img
            cross[pl.ds(s * particles, particles), :] = cross_sum
            noise[pl.ds(s * particles, particles), :] = noise_sum

    total = senders * particles
    rows = [jnp.sum(ref[...].T, axis=0, keepdims=True) for ref in (cross, noise)]
    last.wait()
    rows.append(power[...])
    for d in range(senders):
        for i, row in enumerate(rows):
            out_ref[d, :, i * total : (i + 1) * total] = row


def partial_sums(img, proj, power):
    senders, slices, particles, _ = img.shape
    total = senders * particles
    return pl.pallas_call(
        sums_kernel,
        in_specs=[WHOLE] + [pl.BlockSpec(memory_space=pltpu.HBM)] * 2,
        out_specs=WHOLE,
        out_shape=jax.ShapeDtypeStruct((senders, 1, 3 * total), F32),
        scratch_shapes=[pltpu.VMEM((total, LANES), F32)] * 2
        + [
            pltpu.VMEM(power.shape, F32),
            pltpu.VMEM(proj.shape, F32),
            pltpu.SemaphoreType.DMA((4,)),
            pltpu.SemaphoreType.DMA,
        ],
        compiler_params=params(12),
        cost_estimate=cost(img.size * 4, img.size * 6),
    )(img, in_hbm(proj), in_hbm(power))


def terms_kernel(pixels, part_ref, img_ref, ctf_ref, terms_ref, corr_ref, weight_col):
    senders, slices, particles, _ = img_ref.shape
    total = senders * particles
    sums = part_ref[0]
    for d in range(1, senders):
        sums = sums + part_ref[d]
    cross, power = sums[:, :total], sums[:, 2 * total :]
    noise = sums[:, total : 2 * total] / pixels + EPS
    corr = cross / jnp.sqrt((power + EPS) * noise)
    corr_ref[...] = corr
    weight = jax.nn.sigmoid(corr) / noise
    weight_col[...] = jnp.broadcast_to(weight, (LANES, total)).T

    @pl.loop(0, senders)
    def _(s):
        weight = weight_col[pl.ds(s * particles, particles), :]
        for j in range(slices):
            ctf = ctf_ref[s, j]
            scaled = weight * ctf
            rows = pl.ds(j * particles, particles)
            terms_ref[s, rows, :LANES] = (scaled * img_ref[s, j].astype(F32)).astype(BF16)
            terms_ref[s, rows, LANES:] = (scaled * ctf).astype(BF16)


def make_terms(partials, img, ctf, pixels):
    senders, slices, particles, _ = img.shape
    total = senders * particles
    return pl.pallas_call(
        functools.partial(terms_kernel, float(pixels)),
        in_specs=[WHOLE] * 3,
        out_specs=[WHOLE] * 2,
        out_shape=[
            jax.ShapeDtypeStruct((senders, slices * particles, 2 * LANES), BF16),
            jax.ShapeDtypeStruct((1, total), F32),
        ],
        scratch_shapes=[pltpu.VMEM((total, LANES), F32)],
        compiler_params=params(8),
        cost_estimate=cost(img.size * 4, img.size * 10),
    )(partials, img, in_vmem(ctf))


def scatter_kernel(
    capacity, shift, offsets, at_ref, meta_ref, place_ref, terms_ref, out_ref, sorted_ref
):
    senders, rows, width = terms_ref.shape
    blocks = out_ref.shape[1] * 2 // 3
    owned = blocks // 2
    y = lax.rem(at_ref[0] + shift, RING)
    holders = [y * RING + lax.rem(at_ref[1] + u, RING) for u in offsets]
    place_in = lax.broadcasted_iota(jnp.int32, (capacity, rows), 0)
    slot_at = [(place_in + h * capacity).astype(F32) for h in holders]
    slot_at = jnp.concatenate(slot_at, axis=0)
    for s in range(senders):
        pick = (slot_at == meta_ref[s, :, rows : 2 * rows]).astype(BF16)
        got = jnp.dot(pick, terms_ref[s], preferred_element_type=F32).astype(BF16)
        for i in range(len(offsets)):
            sorted_ref[i, s * capacity : (s + 1) * capacity, :] = got[
                i * capacity : (i + 1) * capacity
            ]
    block_at = lax.broadcasted_iota(jnp.int32, (blocks, senders * capacity), 0).astype(F32)
    for i, h in enumerate(holders):
        one_hot = (block_at == place_ref[h]).astype(BF16)
        summed = jnp.dot(one_hot, sorted_ref[i], preferred_element_type=F32)
        denom = jnp.where(at_ref[2] == 0, summed[:owned, LANES:], summed[owned:, LANES:])
        out_ref[i, :blocks, :] = summed[:, :LANES].astype(out_ref.dtype)
        out_ref[i, blocks:, :] = denom.astype(out_ref.dtype)


def scatter(at, shift, offsets, meta, places, terms, blocks, capacity, kind):
    senders, rows, width = terms.shape
    held = len(offsets)
    out = jax.ShapeDtypeStruct((held, blocks * 3 // 2, LANES), kind)
    return pl.pallas_call(
        functools.partial(scatter_kernel, capacity, shift, offsets),
        in_specs=[SCALARS] + [WHOLE] * 3,
        out_specs=WHOLE,
        out_shape=out,
        scratch_shapes=[pltpu.VMEM((held, senders * capacity, width), BF16)],
        compiler_params=params(12),
        cost_estimate=cost(
            2 * senders * held * capacity * width * (rows + blocks), 5 * MIB
        ),
    )(at, meta, places, terms)


def fold_kernel(own_ref, got1, got2, got3, *outs):
    for i, ref in enumerate(outs):
        total = own_ref[i]
        for got in (got1, got2, got3):
            total = total + got[i].astype(F32)
        ref[...] = total.astype(ref.dtype)


def fold(own, got, kinds):
    _, rows, width = own.shape
    return pl.pallas_call(
        fold_kernel,
        in_specs=[WHOLE] * 4,
        out_specs=[WHOLE] * len(kinds),
        out_shape=[jax.ShapeDtypeStruct((rows, width), k) for k in kinds],
        compiler_params=params(4),
        cost_estimate=cost(own.size * 4, own.size * 11),
    )(own, *got)


def ring(x, axis, size, step, shift):
    def target(i):
        place = i // step % RING
        return i + ((place + shift) % RING - place) * step

    return lax.ppermute(x, axis, [(i, target(i)) for i in range(size)])


def shards(images, defocus, assign, orient, owner, slice_loc, volume):
    owners = lax.axis_size("cls")
    groups = lax.axis_size("dom")
    me = lax.axis_index("dom")
    at = lax.axis_index("cls")
    at_y, at_z = at // RING, at % RING
    particles, image_rows, width = images.shape
    classes, owned, block_len = volume.shape
    slices = owner.shape[1]
    blocks = classes * owned
    rows = slices * particles
    capacity = 5 * rows // (2 * owners)

    at_all = jnp.stack([at_y, at_z, me % 2, me // 2])

    meta = make_meta(
        owner, assign, orient, defocus, slice_loc, capacity, owners, blocks, owned, groups
    )
    meta = lax.all_to_all(meta, "dom", 0, 0, tiled=True)
    piece = piece_of(volume, me).reshape(blocks, LANES)
    near = jnp.stack([piece] + [ring(piece, "cls", owners, 1, t) for t in range(1, RING)])
    img = after(split_images(images, slices), near, meta)
    img = lax.all_to_all(img, "dom", 0, 0, tiled=True)
    vols = [near] + [ring(near, "cls", owners, RING, t) for t in range(1, RING)]

    extent = float(image_rows * image_rows)
    ctf, places = contrast(at_all, meta, slices, particles, owners, capacity, extent)
    proj, power = project(at_all, meta, ctf, vols)
    partial = partial_sums(img, proj, power)
    partial = lax.all_to_all(partial, "dom", 0, 0, tiled=True)
    terms, corr = make_terms(partial, img, ctf, image_rows * width)
    correlation = lax.dynamic_slice_in_dim(corr[0], me * particles, particles)

    parts = {}
    for t in (2, 1, 3, 0):
        kind = BF16 if t else F32
        parts[t] = scatter(at_all, t, (2, 1, 3, 0), meta, places, terms, blocks, capacity, kind)
    got = [ring(parts[t], "cls", owners, RING, t) for t in (2, 1, 3)]
    far, right, left, total = fold(parts[0], got, (BF16, BF16, BF16, F32))
    far = ring(far, "cls", owners, 1, 2)
    right = ring(right, "cls", owners, 1, 1)
    left = ring(left, "cls", owners, 1, 3)
    total = total + far.astype(F32) + right.astype(F32) + left.astype(F32)
    numer, mine = total[:blocks], total[blocks:]
    other = lax.ppermute(mine, "dom", [(i, i ^ 1) for i in range(groups)])
    first = me % 2 == 0
    denom = jnp.concatenate([jnp.where(first, mine, other), jnp.where(first, other, mine)])
    new_volume = numer / (denom + 1.0)
    return (new_volume.reshape(classes, owned, LANES), correlation)


def solution(mesh):
    placed = (
        P(("dom", "cls"), None, None),
        P(("dom", "cls")),
        P(("dom", "cls")),
        P(("dom", "cls")),
        P(("dom", "cls"), None),
        P(),
        P(None, "cls", None),
    )
    return jax.shard_map(
        shards,
        mesh=mesh,
        in_specs=placed,
        out_specs=(P(None, "cls", "dom"), P(("dom", "cls"))),
        check_vma=False,
    )
```

```python
import functools
import jax
import jax.numpy as jnp
from jax import lax
from jax.experimental import pallas as pl
from jax.experimental.pallas import tpu as pltpu
from jax.sharding import PartitionSpec as P

F32 = jnp.float32
BF16 = jnp.bfloat16
LANES = 128
PHASE = 0.3
EPS = 1e-05
MIB = 1024 * 1024
RING = 4
PACK = 16
WHOLE = pl.BlockSpec(memory_space=pltpu.VMEM)
SCALARS = pl.BlockSpec(memory_space=pltpu.SMEM)


def params(mib):
    return pltpu.CompilerParams(vmem_limit_bytes=mib * MIB)


def cost(flops, moved):
    return pl.CostEstimate(flops=flops, bytes_accessed=moved, transcendentals=0)


def in_vmem(x):
    return pltpu.with_memory_space_constraint(x, pltpu.VMEM)


def in_hbm(x):
    return pltpu.with_memory_space_constraint(x, pltpu.HBM)


def piece_kernel(column_ref, vol_hbm, out_ref, sem):
    at = pl.ds(pl.multiple_of(column_ref[0] * LANES, LANES), LANES)
    copy = pltpu.make_async_copy(vol_hbm.at[:, :, at], out_ref, sem)
    copy.start()
    copy.wait()


def piece_of(volume, column):
    classes, owned, _ = volume.shape
    return pl.pallas_call(
        piece_kernel,
        in_specs=[SCALARS, pl.BlockSpec(memory_space=pltpu.HBM)],
        out_specs=WHOLE,
        out_shape=jax.ShapeDtypeStruct((classes, owned, LANES), BF16),
        scratch_shapes=[pltpu.SemaphoreType.DMA],
        compiler_params=params(1),
        cost_estimate=cost(0, 4 * classes * owned * LANES),
    )(column.reshape(1), in_hbm(volume))


def split_kernel(slices, img_ref, out_ref):
    particles, rows, _ = img_ref.shape
    block_rows = out_ref.shape[0] // 2
    together = PACK // block_rows
    size = PACK * PACK
    to = lax.broadcasted_iota(jnp.int32, (size, size), 0)
    come = lax.broadcasted_iota(jnp.int32, (size, size), 1)
    moved = (come == (to % PACK) * PACK + to // PACK).astype(BF16)
    for g in range(rows // PACK):
        for i in range(particles // PACK):
            part = img_ref[i * PACK : (i + 1) * PACK, g * PACK : (g + 1) * PACK, :]
            part = part.reshape(size, 2 * LANES)
            got = jnp.dot(moved, part, preferred_element_type=F32).astype(BF16)
            for k in range(PACK):
                j, b = g * together + k // block_rows, k % block_rows
                for h in range(2):
                    out_ref[2 * b + h, j, i * PACK : (i + 1) * PACK, :] = got[
                        k * PACK : (k + 1) * PACK, h * LANES : (h + 1) * LANES
                    ]


def split_images(images, slices):
    particles, rows, width = images.shape
    block_rows = rows // slices
    steps = 2
    return pl.pallas_call(
        functools.partial(split_kernel, slices),
        grid=(steps,),
        in_specs=[pl.BlockSpec((particles, rows // steps, width), lambda i: (0, i, 0))],
        out_specs=pl.BlockSpec(
            (2 * block_rows, slices // steps, particles, LANES), lambda i: (0, i, 0, 0)
        ),
        out_shape=pltpu.HBM((2 * block_rows, slices, particles, LANES), BF16),
        compiler_params=params(56),
        cost_estimate=cost(2 * images.size * PACK * PACK, images.size * 4),
    )(images)


def meta_kernel(
    capacity, blocks, owned, owner_ref, assign_ref, orient_ref, focus_ref, table_ref, meta_ref
):
    slices, particles = owner_ref.shape
    turns = table_ref.shape[1]
    count = slices * particles
    owners = (meta_ref.shape[2] - 2 * count - LANES) // capacity
    turn = lax.broadcasted_iota(jnp.int32, (turns, particles), 0)
    one_hot = (turn == orient_ref[...]).astype(BF16)
    place = jnp.dot(table_ref[...].astype(F32).astype(BF16), one_hot, preferred_element_type=F32)
    place = place + (assign_ref[...] * owned).astype(F32)
    owner = owner_ref[...].astype(F32)
    owner_row = jnp.concatenate([owner[j : j + 1, :] for j in range(slices)], axis=1)
    place_row = jnp.concatenate([place[j : j + 1, :] for j in range(slices)], axis=1)
    holder = lax.broadcasted_iota(jnp.int32, (owners, count), 0).astype(F32)
    match = (holder == owner_row).astype(BF16)
    before = lax.broadcasted_iota(jnp.int32, (count, count), 0)
    before = before < lax.broadcasted_iota(jnp.int32, (count, count), 1)
    earlier = jnp.dot(match, before.astype(BF16), preferred_element_type=F32)
    rank = jnp.sum(earlier * match.astype(F32), axis=0, keepdims=True)
    slot = owner_row * float(capacity) + rank
    slot_col = jnp.broadcast_to(slot, (8, count)).T[:, :1]
    every = lax.broadcasted_iota(jnp.int32, (count, owners * capacity), 1).astype(F32)
    at_slot = (every == slot_col).astype(BF16)
    shifted = jnp.broadcast_to(place_row + 1.0, (8, count)).astype(BF16)
    filled = jnp.dot(shifted, at_slot, preferred_element_type=F32)[:1] - 1.0
    last = 2 * count + owners * capacity
    tail = jnp.zeros((1, meta_ref.shape[2] - last - particles), F32)
    focus = jnp.concatenate([focus_ref[...].astype(F32), tail], axis=1)
    for d in range(meta_ref.shape[0]):
        meta_ref[d, :, :count] = owner_row * float(blocks) + place_row
        meta_ref[d, :, count : 2 * count] = slot
        meta_ref[d, :, 2 * count : last] = filled
        meta_ref[d, :, last:] = focus


def make_meta(owner, assign, orient, defocus, table, capacity, owners, blocks, owned, copies):
    particles, slices = owner.shape
    length = 2 * slices * particles + owners * capacity + LANES
    return pl.pallas_call(
        functools.partial(meta_kernel, capacity, blocks, owned),
        out_shape=jax.ShapeDtypeStruct((copies, 1, length), F32),
        compiler_params=params(56),
        cost_estimate=cost(100 * MIB, MIB),
    )(owner.T, assign[None, :], orient[None, :], defocus[None, :], table.T)


def after_kernel(x_ref, y_ref, z_ref, out_ref):
    pass


def after(x, y, z):
    hbm = pl.BlockSpec(memory_space=pltpu.HBM)
    anywhere = pl.BlockSpec(memory_space=pl.ANY)
    return pl.pallas_call(
        after_kernel,
        in_specs=[hbm, anywhere, anywhere],
        out_specs=hbm,
        out_shape=pltpu.HBM(x.shape, x.dtype),
        input_output_aliases={0: 0},
        compiler_params=params(1),
    )(x, y, z)


def contrast_kernel(extent, capacity, at_ref, meta_ref, ctf_ref, place_ref):
    held, slices, particles, _ = ctf_ref.shape
    owners = place_ref.shape[0]
    start = meta_ref.shape[2] - LANES
    for k in range(held):
        focus = meta_ref[k, :, start:]
        focus = jnp.broadcast_to(focus, (LANES, LANES)).T[:particles, :] / extent
        column = lax.broadcasted_iota(jnp.int32, (particles, LANES), 1).astype(F32)
        angle = focus * (column * column)
        cos_col, sin_col = jnp.cos(angle), jnp.sin(angle)
        row = column * 8.0 + at_ref[3].astype(F32)
        angle = focus * (row * row) + PHASE
        cos_row, sin_row = jnp.cos(angle), jnp.sin(angle)
        for j in range(slices):
            ctf_ref[k, j] = sin_row[:, j : j + 1] * cos_col + cos_row[:, j : j + 1] * sin_col

    first = start - owners * capacity
    for i in range(place_ref.shape[2] // (held * capacity)):

        @pl.when(pl.program_id(0) == i)
        def _():
            for h in range(owners):
                at = first + h * capacity
                got = [meta_ref[k, :, at : at + capacity] for k in range(held)]
                to = i * held * capacity
                place_ref[h, :, to : to + held * capacity] = jnp.concatenate(got, axis=1)


def contrast(at, meta, slices, particles, owners, capacity, extent):
    senders, _, length = meta.shape
    held = 4
    return pl.pallas_call(
        functools.partial(contrast_kernel, extent, capacity),
        grid=(senders // held,),
        in_specs=[SCALARS, pl.BlockSpec((held, 1, length), lambda i: (i, 0, 0))],
        out_specs=[
            pl.BlockSpec((held, slices, particles, LANES), lambda i: (i, 0, 0, 0)),
            pl.BlockSpec((owners, 1, senders * capacity), lambda i: (0, 0, 0)),
        ],
        out_shape=[
            pltpu.VMEM((senders, slices, particles, LANES), F32),
            jax.ShapeDtypeStruct((owners, 1, senders * capacity), F32),
        ],
        compiler_params=params(12),
        cost_estimate=cost(MIB, MIB),
    )(at, meta)


def project_kernel(
    count, at_ref, meta_ref, ctf_ref, vol0, vol1, vol2, vol3, proj_ref, power_ref, pairs
):
    taken, slices, particles, _ = proj_ref.shape
    held, blocks, _ = vol0.shape
    owned = blocks // 2
    holders = RING * held

    @pl.when(pl.program_id(0) == 0)
    def _():
        for t, vol in enumerate((vol0, vol1, vol2, vol3)):
            for i in range(held):
                where = pl.ds((t * held + i) * owned, owned)
                pairs[where, :LANES] = vol[i, :owned, :]
                pairs[where, LANES:] = vol[i, owned:, :]

    at_y = at_ref[0].astype(F32)
    at_z = at_ref[1].astype(F32)
    lane = lax.broadcasted_iota(jnp.int32, (count, LANES), 1).astype(F32)
    zero = jnp.zeros((count, owned), BF16)
    powers = []
    for k in range(taken):
        key = meta_ref[k, :, :count]
        owner = jnp.floor(key * (1.0 / blocks))
        place = key - owner * float(blocks)
        upper = (place >= float(owned)).astype(F32)
        place = place - upper * float(owned)
        y = jnp.floor(owner * (1.0 / held))
        z = at_z - (owner - y * float(held))
        y = at_y - y
        y = jnp.where(y < 0.0, y + float(RING), y)
        z = jnp.where(z < 0.0, z + float(RING), z)
        rows = jnp.concatenate([place] * 8 + [upper] * 8 + [y * float(held) + z] * 8, axis=0).T
        hit = jnp.broadcast_to(rows[:, :1], (count, LANES)) == lane
        hit = hit.astype(BF16)
        upper = jnp.broadcast_to(rows[:, 8:9], (count, LANES)) > 0.5
        holder = jnp.broadcast_to(rows[:, 16:17], (count, LANES)).astype(BF16)
        acc = jnp.zeros((count, 2 * LANES), F32)
        for i in range(0, holders, held):
            one_hot = [jnp.where(holder == i + q, hit, zero) for q in range(held)]
            one_hot = jnp.concatenate(one_hot, axis=1)
            some = pairs[i * owned : (i + held) * owned, :]
            acc += jnp.dot(one_hot, some, preferred_element_type=F32)
        picked = jnp.where(upper, acc[:, LANES:], acc[:, :LANES])
        picked = picked.reshape(slices, particles, LANES)
        power = jnp.zeros((particles, LANES), F32)
        for j in range(slices):
            proj = ctf_ref[k, j] * picked[j]
            power += proj * proj
            proj_ref[k, j] = proj
        powers.append(power)
    power_ref[...] = jnp.sum(jnp.concatenate(powers, axis=0).T, axis=0, keepdims=True)


def project(at, meta, ctf, vols):
    senders, slices, particles, _ = ctf.shape
    held, blocks, _ = vols[0].shape
    span = RING * held * blocks // 2
    count = slices * particles
    taken = 4
    block = pl.BlockSpec((taken, slices, particles, LANES), lambda i: (i, 0, 0, 0))
    return pl.pallas_call(
        functools.partial(project_kernel, count),
        grid=(senders // taken,),
        in_specs=[
            SCALARS,
            pl.BlockSpec((taken, 1, meta.shape[2]), lambda i: (i, 0, 0)),
            block,
        ]
        + [pl.BlockSpec((held, blocks, LANES), lambda i: (0, 0, 0))] * RING,
        out_specs=[block, pl.BlockSpec((1, taken * particles), lambda i: (0, i))],
        out_shape=[
            pltpu.HBM(ctf.shape, F32),
            jax.ShapeDtypeStruct((1, senders * particles), F32),
        ],
        scratch_shapes=[pltpu.VMEM((span, 2 * LANES), BF16)],
        compiler_params=params(20),
        cost_estimate=cost(5 * 2 * senders * count * span * 2 * LANES, 10 * MIB),
    )(at, meta, in_vmem(ctf), *vols)


def fetch(src, dst, sems):
    parts = sems.shape[0]
    size = src.shape[0] // parts
    copies = []
    for i in range(parts):
        at = pl.ds(i * size, size)
        copies.append(pltpu.make_async_copy(src.at[at], dst.at[at], sems.at[i]))
        copies[-1].start()
    return copies


def sums_kernel(img_ref, proj_hbm, power_hbm, out_ref, cross, noise, power, proj, sems, sem):
    senders, slices, particles, _ = img_ref.shape
    copies = fetch(proj_hbm, proj, sems)
    last = pltpu.make_async_copy(power_hbm, power, sem)
    last.start()
    size = senders // len(copies)
    total = senders * particles

    def put(i, row):
        for d in range(senders):
            out_ref[d, :, i * total : (i + 1) * total] = row

    @pl.loop(0, senders)
    def _(s):
        noise_sum = jnp.zeros((particles, LANES), F32)
        for j in range(slices):
            img = img_ref[s, j].astype(F32)
            noise_sum += img * img
        noise[pl.ds(s * particles, particles), :] = noise_sum

    put(1, jnp.sum(noise[...].T, axis=0, keepdims=True))
    last.wait()
    put(2, power[...])
    for i, copy in enumerate(copies):
        copy.wait()

        @pl.loop(i * size, (i + 1) * size)
        def _(s):
            cross_sum = jnp.zeros((particles, LANES), F32)
            for j in range(slices):
                cross_sum += img_ref[s, j].astype(F32) * proj[s, j]
            cross[pl.ds(s * particles, particles), :] = cross_sum

    put(0, jnp.sum(cross[...].T, axis=0, keepdims=True))


def partial_sums(img, proj, power):
    senders, slices, particles, _ = img.shape
    total = senders * particles
    return pl.pallas_call(
        sums_kernel,
        in_specs=[WHOLE] + [pl.BlockSpec(memory_space=pltpu.HBM)] * 2,
        out_specs=WHOLE,
        out_shape=jax.ShapeDtypeStruct((senders, 1, 3 * total), F32),
        scratch_shapes=[pltpu.VMEM((total, LANES), F32)] * 2
        + [
            pltpu.VMEM(power.shape, F32),
            pltpu.VMEM(proj.shape, F32),
            pltpu.SemaphoreType.DMA((8,)),
            pltpu.SemaphoreType.DMA,
        ],
        compiler_params=params(12),
        cost_estimate=cost(img.size * 4, img.size * 6),
    )(img, in_hbm(proj), in_hbm(power))


def terms_kernel(pixels, part_ref, img_ref, ctf_ref, terms_ref, corr_ref, weight_col):
    senders, slices, particles, _ = img_ref.shape
    total = senders * particles
    sums = part_ref[0]
    for d in range(1, senders):
        sums = sums + part_ref[d]
    cross, power = sums[:, :total], sums[:, 2 * total :]
    noise = sums[:, total : 2 * total] / pixels + EPS
    corr = cross / jnp.sqrt((power + EPS) * noise)
    corr_ref[...] = corr
    weight = jax.nn.sigmoid(corr) / noise
    weight_col[...] = jnp.broadcast_to(weight, (LANES, total)).T

    @pl.loop(0, senders)
    def _(s):
        weight = weight_col[pl.ds(s * particles, particles), :]
        for j in range(slices):
            ctf = ctf_ref[s, j]
            scaled = weight * ctf
            rows = pl.ds(j * particles, particles)
            terms_ref[s, rows, :LANES] = (scaled * img_ref[s, j].astype(F32)).astype(BF16)
            terms_ref[s, rows, LANES:] = (scaled * ctf).astype(BF16)


def make_terms(partials, img, ctf, pixels):
    senders, slices, particles, _ = img.shape
    total = senders * particles
    return pl.pallas_call(
        functools.partial(terms_kernel, float(pixels)),
        in_specs=[WHOLE] * 3,
        out_specs=[WHOLE] * 2,
        out_shape=[
            jax.ShapeDtypeStruct((senders, slices * particles, 2 * LANES), BF16),
            jax.ShapeDtypeStruct((1, total), F32),
        ],
        scratch_shapes=[pltpu.VMEM((total, LANES), F32)],
        compiler_params=params(8),
        cost_estimate=cost(img.size * 4, img.size * 10),
    )(partials, img, in_vmem(ctf))


def scatter_kernel(
    capacity, shift, offsets, at_ref, meta_ref, place_ref, terms_ref, out_ref, sorted_ref
):
    senders, rows, width = terms_ref.shape
    blocks = out_ref.shape[1] * 2 // 3
    owned = blocks // 2
    y = lax.rem(at_ref[0] + shift, RING)
    holders = [y * RING + lax.rem(at_ref[1] + u, RING) for u in offsets]
    place_in = lax.broadcasted_iota(jnp.int32, (capacity, rows), 0)
    slot_at = [(place_in + h * capacity).astype(F32) for h in holders]
    slot_at = jnp.concatenate(slot_at, axis=0)
    for s in range(senders):
        pick = (slot_at == meta_ref[s, :, rows : 2 * rows]).astype(BF16)
        got = jnp.dot(pick, terms_ref[s], preferred_element_type=F32).astype(BF16)
        for i in range(len(offsets)):
            sorted_ref[i, s * capacity : (s + 1) * capacity, :] = got[
                i * capacity : (i + 1) * capacity
            ]
    block_at = lax.broadcasted_iota(jnp.int32, (blocks, senders * capacity), 0).astype(F32)
    for i, h in enumerate(holders):
        one_hot = (block_at == place_ref[h]).astype(BF16)
        summed = jnp.dot(one_hot, sorted_ref[i], preferred_element_type=F32)
        denom = jnp.where(at_ref[2] == 0, summed[:owned, LANES:], summed[owned:, LANES:])
        out_ref[i, :blocks, :] = summed[:, :LANES].astype(out_ref.dtype)
        out_ref[i, blocks:, :] = denom.astype(out_ref.dtype)


def scatter(at, shift, offsets, meta, places, terms, blocks, capacity, kind):
    senders, rows, width = terms.shape
    held = len(offsets)
    out = jax.ShapeDtypeStruct((held, blocks * 3 // 2, LANES), kind)
    return pl.pallas_call(
        functools.partial(scatter_kernel, capacity, shift, offsets),
        in_specs=[SCALARS] + [WHOLE] * 3,
        out_specs=WHOLE,
        out_shape=out,
        scratch_shapes=[pltpu.VMEM((held, senders * capacity, width), BF16)],
        compiler_params=params(12),
        cost_estimate=cost(
            2 * senders * held * capacity * width * (rows + blocks), 5 * MIB
        ),
    )(at, meta, places, terms)


def fold_kernel(own_ref, got1, got2, got3, *outs):
    for i, ref in enumerate(outs):
        total = own_ref[i]
        for got in (got1, got2, got3):
            total = total + got[i].astype(F32)
        ref[...] = total.astype(ref.dtype)


def fold(own, got, kinds):
    _, rows, width = own.shape
    return pl.pallas_call(
        fold_kernel,
        in_specs=[WHOLE] * 4,
        out_specs=[WHOLE] * len(kinds),
        out_shape=[jax.ShapeDtypeStruct((rows, width), k) for k in kinds],
        compiler_params=params(4),
        cost_estimate=cost(own.size * 4, own.size * 11),
    )(own, *got)


def ring(x, axis, size, step, shift):
    def target(i):
        place = i // step % RING
        return i + ((place + shift) % RING - place) * step

    return lax.ppermute(x, axis, [(i, target(i)) for i in range(size)])


def shards(images, defocus, assign, orient, owner, slice_loc, volume):
    owners = lax.axis_size("cls")
    groups = lax.axis_size("dom")
    me = lax.axis_index("dom")
    at = lax.axis_index("cls")
    at_y, at_z = at // RING, at % RING
    particles, image_rows, width = images.shape
    classes, owned, block_len = volume.shape
    slices = owner.shape[1]
    blocks = classes * owned
    rows = slices * particles
    capacity = 5 * rows // (2 * owners)

    at_all = jnp.stack([at_y, at_z, me % 2, me // 2])

    meta = make_meta(
        owner, assign, orient, defocus, slice_loc, capacity, owners, blocks, owned, groups
    )
    meta = lax.all_to_all(meta, "dom", 0, 0, tiled=True)
    piece = piece_of(volume, me).reshape(blocks, LANES)
    near = jnp.stack([piece] + [ring(piece, "cls", owners, 1, t) for t in range(1, RING)])
    img = after(split_images(images, slices), near, meta)
    img = lax.all_to_all(img, "dom", 0, 0, tiled=True)
    vols = [near] + [ring(near, "cls", owners, RING, t) for t in range(1, RING)]

    extent = float(image_rows * image_rows)
    ctf, places = contrast(at_all, meta, slices, particles, owners, capacity, extent)
    proj, power = project(at_all, meta, ctf, vols)
    partial = partial_sums(img, proj, power)
    partial = lax.all_to_all(partial, "dom", 0, 0, tiled=True)
    terms, corr = make_terms(partial, img, ctf, image_rows * width)
    correlation = lax.dynamic_slice_in_dim(corr[0], me * particles, particles)

    parts = {}
    for t in (2, 1, 3, 0):
        kind = BF16 if t else F32
        parts[t] = scatter(at_all, t, (2, 1, 3, 0), meta, places, terms, blocks, capacity, kind)
    got = [ring(parts[t], "cls", owners, RING, t) for t in (2, 1, 3)]
    far, right, left, total = fold(parts[0], got, (BF16, BF16, BF16, F32))
    far = ring(far, "cls", owners, 1, 2)
    right = ring(right, "cls", owners, 1, 1)
    left = ring(left, "cls", owners, 1, 3)
    total = total + far.astype(F32) + right.astype(F32) + left.astype(F32)
    numer, mine = total[:blocks], total[blocks:]
    other = lax.ppermute(mine, "dom", [(i, i ^ 1) for i in range(groups)])
    first = me % 2 == 0
    denom = jnp.concatenate([jnp.where(first, mine, other), jnp.where(first, other, mine)])
    new_volume = numer / (denom + 1.0)
    return (new_volume.reshape(classes, owned, LANES), correlation)


def solution(mesh):
    placed = (
        P(("dom", "cls"), None, None),
        P(("dom", "cls")),
        P(("dom", "cls")),
        P(("dom", "cls")),
        P(("dom", "cls"), None),
        P(),
        P(None, "cls", None),
    )
    return jax.shard_map(
        shards,
        mesh=mesh,
        in_specs=placed,
        out_specs=(P(None, "cls", "dom"), P(("dom", "cls"))),
        check_vma=False,
    )
```
